32 devices in a mesh: seq: 8 (over z, y), head: 4 (over x, core).
Axes of the slice: x: 2, y: 2, z: 4, core: 2. Of those that a mesh axis runs over, the one named last changes fastest.
Arguments:
- queries: bfloat16 [16384, 4096], P('seq', 'head'), may hold values from -5 to 5
- keys: bfloat16 [16384, 1024], P('seq', 'head'), may hold values from -5 to 5
- values: bfloat16 [16384, 1024], P('seq', 'head'), may hold values from -6 to 6
- grad_out: bfloat16 [16384, 4096], P('seq', 'head'), may hold values from -6 to 6
- vertical: int32 [8], replicated, may hold values from 0 to 15
- columns: int32 [128, 2], P('seq'), may hold values from 0 to 7, as said below
- offsets: int32 [128, 2], P('seq'), may hold values from 1 to 32
Outputs:
- grad_queries: bfloat16 [16384, 4096], P(('seq', 'head'))
- grad_keys: bfloat16 [16384, 1024], P(('seq', 'head'))
- grad_values: bfloat16 [16384, 1024], P(('seq', 'head'))
The draws below stay inside these ranges and needn't reach their ends.
Inputs may be any that keep to these rules, and one draw needn't show every extreme that they name: `columns`: entry c names vertical column c, held by seq index c; an entry of query block i is below (i // 16 + 1).
All inputs are finite; a program needn't handle non-finite values.
Results may differ from the reference program's by a relative error of at most 0.014.
Values may be sent and summed in bfloat16 or wider, within the bound.
No kernel may reach another device: no remote copies, remote signals or barrier semaphores. Data moves between devices by JAX's collectives and lax.ppermute only.
A program may use at most 192 MiB of HBM per device.

```python
import math
import jax
import jax.numpy as jnp
from jax import lax

H = 32
KVH = 8
HD = 128
BLK = 128
VERT_DEV = 1
TOK_DEV = 2048
TOKENS = 16384
NB = 128
NV = 8


def base_field(key, width):
    return jnp.clip(jax.random.normal(key, (TOKENS, width), jnp.float32), -5.0, 5.0)


def draw_queries(key, part):
    field = base_field(jax.random.fold_in(key, 11), H * HD)
    return field.astype(jnp.bfloat16)


def draw_keys(key, part):
    field = base_field(jax.random.fold_in(key, 12), KVH * HD)
    return field.astype(jnp.bfloat16)


def draw_columns(key, part):
    rows = jnp.arange(NB)
    upper = (rows // (TOK_DEV // BLK) + 1) * VERT_DEV
    return jax.random.randint(key, (NB, 2), 0, upper[:, None]).astype(jnp.int32)


def place_ends(entries, key, smallest, largest):
    extent = entries.shape
    spot = [jax.random.randint(jax.random.fold_in(key, axis), (), 0, extent[axis]) for axis in range(len(extent))]
    entries = entries.at[tuple(spot)].set(smallest)
    longest = extent.index(max(extent))
    spot[longest] = (spot[longest] + 1) % extent[longest]
    return entries.at[tuple(spot)].set(largest)


def steps_of(key, shape, pieces, low, largest):
    level = 1.0
    for axis_at, parts in pieces:
        steps = jax.random.uniform(jax.random.fold_in(jax.random.fold_in(key, 6), axis_at), (parts,), jnp.float32, low / len(pieces), largest / len(pieces))
        level = level * jnp.repeat(jnp.exp(steps), shape[axis_at] // parts).reshape((-1,) + (1,) * (len(shape) - 1 - axis_at))
    return level


def centred(own_key, shape, spread, reach, pieces=(), kind=jnp.bfloat16):
    drawn = jax.random.normal(own_key, shape, jnp.float32) * spread
    if len(pieces) > 0:
        drawn = steps_of(own_key, shape, pieces, -0.22, 0.18) * drawn
    return jnp.clip(drawn, min=-reach, max=reach).astype(kind)


def setup_inputs(seed: int = 0) -> dict:
    streams_of = jax.random.split(jax.random.key(seed), 8)
    queries = draw_queries(jax.random.fold_in(streams_of[7], 71), 0)
    keys = draw_keys(jax.random.fold_in(streams_of[7], 71), 0)
    values = centred(streams_of[2], (TOKENS, KVH * HD), 1.0, 6.0, ((0, 8), (1, 4)))
    grad_out = centred(streams_of[3], (TOKENS, H * HD), 1.0, 6.0, ((0, 8), (1, 4)))
    vertical = place_ends(jax.random.randint(streams_of[4], (NV,), 0, TOK_DEV // BLK), jax.random.fold_in(streams_of[4], 1), 0, (TOK_DEV // BLK) - 1).astype(jnp.int32)
    columns = draw_columns(jax.random.fold_in(streams_of[7], 71), 0)
    offsets = place_ends(jax.random.randint(streams_of[6], (NB, 2), 1, 2 * (TOK_DEV // BLK) + 1), jax.random.fold_in(streams_of[6], 1), 1, (2 * (TOK_DEV // BLK) + 1) - 1).astype(jnp.int32)
    return {"queries": queries, "keys": keys, "values": values, "grad_out": grad_out, "vertical": vertical, "columns": columns, "offsets": offsets}


def reference(queries, keys, values, grad_out, vertical, columns, offsets):
    tokens = queries.shape[0]
    block_count = tokens // BLK
    local_blocks = TOK_DEV // BLK
    group_size = H // KVH
    score_scale = 1.0 / math.sqrt(HD)
    query_blocks = queries.reshape(block_count, BLK, KVH, group_size, HD)
    grad_blocks = grad_out.reshape(block_count, BLK, KVH, group_size, HD)
    key_blocks = keys.reshape(block_count, BLK, KVH, HD)
    value_blocks = values.reshape(block_count, BLK, KVH, HD)
    vert_ids = jnp.arange(vertical.shape[0], dtype=jnp.int32)
    vert_global = (vert_ids // VERT_DEV * local_blocks + vertical).astype(jnp.int32)
    positions = jnp.arange(BLK)
    causal = positions[None, :] <= positions[:, None]

    def block_step(accums, block_index):
        acc_keys, acc_values = accums
        block_index = block_index.astype(jnp.int32)
        slot_blocks = jnp.stack([jnp.zeros((), jnp.int32), block_index, block_index - offsets[block_index, 0], block_index - offsets[block_index, 1], vert_global[columns[block_index, 0]], vert_global[columns[block_index, 1]]]).astype(jnp.int32)
        slot_flags = []
        for slot_number in range(6):
            current = slot_blocks[slot_number]
            slot_good = (current >= 0) & (current <= block_index)
            for prior in range(slot_number):
                slot_good = slot_good & (current != slot_blocks[prior])
            slot_flags.append(slot_good)
        slot_valid = jnp.stack(slot_flags)
        safe_blocks = jnp.clip(slot_blocks, 0, block_count - 1).astype(jnp.int32)
        key_rows = key_blocks[safe_blocks].astype(jnp.float32)
        value_rows = value_blocks[safe_blocks].astype(jnp.float32)
        query_rows = query_blocks[block_index].astype(jnp.float32)
        grad_rows = grad_blocks[block_index].astype(jnp.float32)
        scores = jnp.einsum('qkgd,sckd->kgqsc', query_rows, key_rows) * score_scale
        earlier = slot_blocks < block_index
        visible = slot_valid[None, :, None] & (earlier[None, :, None] | causal[:, None, :])
        visible = visible[None, None]
        masked = jnp.where(visible, scores, -1e+30)
        row_top = lax.optimization_barrier(jnp.max(masked, axis=(3, 4), keepdims=True))
        row_total = lax.optimization_barrier(jnp.sum(jnp.where(visible, jnp.exp(masked - row_top), 0.0), axis=(3, 4), keepdims=True))
        prob_full = jnp.where(visible, jnp.exp(masked - (row_top + jnp.log(row_total))), 0.0)
        grad_prob = jnp.einsum('qkgd,sckd->kgqsc', grad_rows, value_rows)
        row_delta = lax.optimization_barrier(jnp.sum(prob_full * grad_prob, axis=(3, 4), keepdims=True))
        dscore = (prob_full * (grad_prob - row_delta) * score_scale).astype(jnp.bfloat16)
        prob_half = prob_full.astype(jnp.bfloat16)
        grad_query = jnp.einsum('kgqsc,sckd->qkgd', dscore.astype(jnp.float32), key_rows).astype(jnp.bfloat16)
        key_terms = jnp.einsum('kgqsc,qkgd->sckd', dscore.astype(jnp.float32), query_rows)
        value_terms = jnp.einsum('kgqsc,qkgd->sckd', prob_half.astype(jnp.float32), grad_rows)
        acc_keys = acc_keys.at[safe_blocks].add(key_terms)
        acc_values = acc_values.at[safe_blocks].add(value_terms)
        return ((acc_keys, acc_values), grad_query)
    zero_acc = jnp.zeros((block_count, BLK, KVH, HD), jnp.float32)
    (acc_keys, acc_values), grad_query = lax.scan(block_step, (zero_acc, zero_acc), jnp.arange(block_count, dtype=jnp.int32))
    grad_queries = grad_query.reshape(tokens, H * HD)
    grad_keys = acc_keys.reshape(tokens, KVH * HD).astype(jnp.bfloat16)
    grad_values = acc_values.reshape(tokens, KVH * HD).astype(jnp.bfloat16)
    return (grad_queries, grad_keys, grad_values)
```

```python
import functools
import math

import jax
import jax.numpy as jnp
from jax import lax
from jax.experimental import pallas as pl
from jax.experimental.pallas import tpu as pltpu
from jax.sharding import PartitionSpec as P

HD = 128
BLK = 128
VERT_DEV = 1
FAR = 1e30


def attention_kernel(
    dims, place, vertical, columns, offsets, q_ref, do_ref, kv_own, kv_back, kv_even, kv_odd, kv_far,
    dq_ref, own_ref, prev_ref, back_ref, far_ref, pool_k, pool_v, acc_k, acc_v, sems,
):
    local_blocks, group, vert_total = dims
    step = pl.program_id(0)
    seq_index = place[0]
    rows = local_blocks * BLK
    far_rows = (vert_total + 1) * BLK
    total_rows = 3 * rows + far_rows
    scale = 1.0 / math.sqrt(HD)

    @pl.when(step == 0)
    def _():
        def copies(prev):
            made = []
            for side, pool in enumerate((pool_k, pool_v)):
                for number, (source, start, size) in enumerate(
                    ((kv_own, 0, rows), (prev, rows, rows), (kv_back, 2 * rows, rows), (kv_far, 3 * rows, far_rows))
                ):
                    made.append(
                        pltpu.make_async_copy(
                            source.at[side], pool.at[pl.ds(start, size)], sems.at[side * 4 + number]
                        )
                    )
            return made

        odd = lax.rem(seq_index, 2) == 1

        @pl.when(odd)
        def _():
            for copy in copies(kv_even):
                copy.start()

        @pl.when(jnp.logical_not(odd))
        def _():
            for copy in copies(kv_odd):
                copy.start()

        acc_k[...] = jnp.zeros_like(acc_k)
        acc_v[...] = jnp.zeros_like(acc_v)
        for copy in copies(kv_even):
            copy.wait()

    block = seq_index * local_blocks + step

    def column_block(column):
        return column // VERT_DEV * local_blocks + vertical[column]

    def near(offset):
        at = step - offset
        return jnp.where(at >= 0, at, jnp.where(at >= -local_blocks, at + 2 * local_blocks, at + 4 * local_blocks))

    first, second = offsets[step, 0], offsets[step, 1]
    left, right = columns[step, 0], columns[step, 1]
    b2, b3 = block - first, block - second
    b4, b5 = column_block(left), column_block(right)
    slots = [3 * local_blocks + vert_total, step, near(first), near(second), 3 * local_blocks + left, 3 * local_blocks + right]
    live = [
        block > 0,
        None,
        b2 > 0,
        (b3 > 0) & (b3 != b2),
        (b4 > 0) & (b4 < block) & (b4 != b2) & (b4 != b3),
        (b5 > 0) & (b5 < block) & (b5 != b2) & (b5 != b3) & (b5 != b4),
    ]
    spots = [pl.ds(pl.multiple_of(slot * BLK, BLK), BLK) for slot in slots]
    queries = jnp.concatenate([q_ref[:, g * HD : (g + 1) * HD] for g in range(group)], axis=0)
    grads = jnp.concatenate([do_ref[:, g * HD : (g + 1) * HD] for g in range(group)], axis=0)
    width = group * BLK
    keys = [pool_k[spot, :] for spot in spots]
    values = [pool_v[spot, :] for spot in spots]
    contract_last = (((1,), (1,)), ((), ()))
    contract_first = (((0,), (0,)), ((), ()))
    key_at = lax.broadcasted_iota(jnp.int32, (BLK, width), 0)
    query_at = lax.broadcasted_iota(jnp.int32, (BLK, width), 1) % BLK
    seen = key_at <= query_at
    turn = scale * math.log2(math.e)
    scores, tops = [], []
    for number in range(6):
        part = lax.dot_general(keys[number], queries, contract_last, preferred_element_type=jnp.float32)
        part = part * turn
        if number == 1:
            part = jnp.where(seen, part, -FAR)
        scores.append(part)
        top = jnp.max(part, axis=0, keepdims=True)
        if number != 1:
            top = jnp.where(live[number], top, -FAR)
        tops.append(top)
    top = functools.reduce(jnp.maximum, tops)
    weights, products = [], []
    total = jnp.zeros((1, width), jnp.float32)
    delta = jnp.zeros((1, width), jnp.float32)
    for number in range(6):
        base = top if number == 1 else jnp.where(live[number], top, FAR)
        weight = jnp.exp2(scores[number] - base)
        product = lax.dot_general(values[number], grads, contract_last, preferred_element_type=jnp.float32)
        total = total + jnp.sum(weight, axis=0, keepdims=True)
        delta = delta + jnp.sum(weight * product, axis=0, keepdims=True)
        weights.append(weight)
        products.append(product)
    inverse = 1.0 / total
    delta = delta * inverse
    dq = jnp.zeros((width, HD), jnp.float32)
    for number in range(6):
        prob = weights[number] * inverse
        dscore = (prob * (products[number] - delta)).astype(jnp.bfloat16)
        prob = prob.astype(jnp.bfloat16)
        acc_v[spots[number], :] += jnp.dot(prob, grads, preferred_element_type=jnp.float32)
        acc_k[spots[number], :] += jnp.dot(dscore, queries, preferred_element_type=jnp.float32)
        dq = dq + lax.dot_general(dscore, keys[number], contract_first, preferred_element_type=jnp.float32)
    dq = (dq * scale).astype(dq_ref.dtype)
    for g in range(group):
        dq_ref[:, g * HD : (g + 1) * HD] = dq[g * BLK : (g + 1) * BLK]

    @pl.when(step == local_blocks - 1)
    def _():
        for side, (acc, factor) in enumerate(((acc_k, scale), (acc_v, 1.0))):
            own_ref[side] = acc[:rows, :] * factor
            prev_ref[side] = (acc[rows : 2 * rows, :] * factor).astype(prev_ref.dtype)
            back_ref[side] = (acc[2 * rows : 3 * rows, :] * factor).astype(back_ref.dtype)
            far_ref[side] = (acc[3 * rows :, :] * factor).astype(far_ref.dtype)


def attention(head, kv_local, place, vertical, columns, offsets, queries, grad_out, kv_own, kv_back, kv_even, kv_odd, kv_far):
    seq_len = queries.shape[0]
    local_blocks = seq_len // BLK
    width = queries.shape[1] // kv_local
    group = width // HD
    vert_total = vertical.shape[0]
    far_rows = (vert_total + 1) * BLK
    total_rows = 3 * seq_len + far_rows
    anywhere = pl.BlockSpec(memory_space=pl.ANY)
    by_block = pl.BlockSpec((BLK, width), lambda i, *_: (i, head))

    def whole(*shape):
        return pl.BlockSpec(shape, lambda i, *_: (0,) * len(shape))

    near_shape = (2, seq_len, HD)
    far_shape = (2, far_rows, HD)
    flops = 2 * 5 * seq_len * group * 6 * BLK * HD
    return pl.pallas_call(
        functools.partial(attention_kernel, (local_blocks, group, vert_total)),
        grid_spec=pltpu.PrefetchScalarGridSpec(
            num_scalar_prefetch=4,
            grid=(local_blocks,),
            in_specs=[by_block, by_block] + [anywhere] * 5,
            out_specs=[
                pl.BlockSpec((BLK, width), lambda i, *_: (i, 0)),
                whole(*near_shape), whole(*near_shape), whole(*near_shape), whole(*far_shape),
            ],
            scratch_shapes=[
                pltpu.VMEM((total_rows, HD), jnp.bfloat16),
                pltpu.VMEM((total_rows, HD), jnp.bfloat16),
                pltpu.VMEM((total_rows, HD), jnp.float32),
                pltpu.VMEM((total_rows, HD), jnp.float32),
                pltpu.SemaphoreType.DMA((8,)),
            ],
        ),
        out_shape=[
            jax.ShapeDtypeStruct((seq_len, width), jnp.bfloat16),
            jax.ShapeDtypeStruct(near_shape, jnp.float32),
            jax.ShapeDtypeStruct(near_shape, jnp.bfloat16),
            jax.ShapeDtypeStruct(near_shape, jnp.bfloat16),
            jax.ShapeDtypeStruct(far_shape, jnp.bfloat16),
        ],
        compiler_params=pltpu.CompilerParams(vmem_limit_bytes=50 * 1024 * 1024),
        cost_estimate=pl.CostEstimate(flops=flops, bytes_accessed=20 * 1024 * 1024, transcendentals=seq_len * group * 6 * BLK),
        name="attention",
    )(place, vertical, columns, offsets, queries, grad_out, kv_own, kv_back, kv_even, kv_odd, kv_far)


def assemble_kernel(heads, kv_local, place, *refs):
    count = heads * kv_local
    outs = refs[3 * count :]
    for number, out in enumerate(outs):
        for at in range(count):
            piece = refs[number * count + at]
            width = piece.shape[1]
            source = place[1] ^ (at // kv_local)
            start = pl.multiple_of((source * kv_local + at % kv_local) * width, width)
            out[:, pl.ds(start, width)] = piece[...]


def assemble(place, heads, query_pieces, key_pieces, value_pieces):
    groups = (query_pieces, key_pieces, value_pieces)
    count = len(query_pieces)
    rows = query_pieces[0].shape[0]
    tile = min(rows, 128)

    def spec(width):
        return pl.BlockSpec((tile, width), lambda i, *_: (i, 0))

    return pl.pallas_call(
        functools.partial(assemble_kernel, heads, count // heads),
        grid_spec=pltpu.PrefetchScalarGridSpec(
            num_scalar_prefetch=1,
            grid=(rows // tile,),
            in_specs=[spec(piece.shape[1]) for group in groups for piece in group],
            out_specs=[spec(group[0].shape[1] * count) for group in groups],
        ),
        out_shape=[jax.ShapeDtypeStruct((rows, group[0].shape[1] * count), group[0].dtype) for group in groups],
        name="assemble",
    )(place, *(piece for group in groups for piece in group))


def shards(queries, keys, values, grad_out, vertical, columns, offsets):
    seq_len = queries.shape[0]
    seq_size = lax.axis_size("seq")
    head_size = lax.axis_size("head")
    kv_local = keys.shape[1] // HD
    seq_index = lax.axis_index("seq")
    head_index = lax.axis_index("head")
    place = jnp.stack([seq_index, head_index]).astype(jnp.int32)
    odd = seq_index % 2 == 1
    evens = range(0, seq_size, 2)

    def along(array, pairs):
        return lax.ppermute(array, "seq", pairs)

    forward = [(i, i + 2) for i in range(seq_size - 2)]
    backward = [(i + 2, i) for i in range(seq_size - 2)]
    exchange = [(i, i ^ 1) for i in range(seq_size)]
    even_to_odd = [(i, i + 1) for i in evens]
    odd_to_even = [(i + 1, i) for i in evens]
    steps = int(math.log2(seq_size))
    own_vertical = lax.dynamic_slice_in_dim(vertical, seq_index * VERT_DEV, VERT_DEV)

    def spread(kv):
        mine = lax.dynamic_slice_in_dim(kv, own_vertical[0] * BLK, BLK, axis=1)
        sink = kv[:, :BLK]
        held = mine
        for level in range(steps):
            hop = 1 << level
            got = along(jnp.concatenate([held, sink], axis=1), [(i, i ^ hop) for i in range(seq_size)])
            got_held, got_sink = got[:, :-BLK], got[:, -BLK:]
            upper = (seq_index & hop) != 0
            held = jnp.where(upper, jnp.concatenate([got_held, held], axis=1), jnp.concatenate([held, got_held], axis=1))
            sink = jnp.where(seq_index < hop, sink, got_sink)
        return jnp.concatenate([held, sink], axis=1)

    def collect(far):
        held, sink = far[:, :-BLK].astype(jnp.float32), far[:, -BLK:].astype(jnp.float32)
        for level in reversed(range(steps)):
            hop = 1 << level
            size = held.shape[1] // 2
            upper = (seq_index & hop) != 0
            low, high = held[:, :size], held[:, size:]
            sent = jnp.concatenate([jnp.where(upper, low, high), sink], axis=1).astype(jnp.bfloat16)
            got = along(sent, [(i, i ^ hop) for i in range(seq_size)]).astype(jnp.float32)
            held = jnp.where(upper, high, low) + got[:, :size]
            sink = sink + got[:, size:]
        return held, sink

    query_pieces, key_pieces, value_pieces = {}, {}, {}

    def to_tokens(array, k, axis):
        size = array.shape[axis] // head_size
        piece = lax.dynamic_slice_in_dim(array, (head_index ^ k) * size, size, axis=axis)
        if k == 0:
            return piece
        return lax.ppermute(piece, "head", [(i, i ^ k) for i in range(head_size)])

    for head in range(kv_local):
        span = slice(head * HD, (head + 1) * HD)
        kv = jnp.stack([keys[:, span], values[:, span]])
        kv_even = along(kv, even_to_odd)
        kv_back = along(kv, forward)
        kv_odd = along(kv_back, odd_to_even)
        kv_far = spread(kv)
        dq, own, prev, back, far = attention(
            head, kv_local, place, vertical, columns, offsets, queries, grad_out, kv, kv_back, kv_even, kv_odd, kv_far
        )
        for k in range(head_size):
            query_pieces[k, head] = to_tokens(dq, k, 0)
        side = along(prev, exchange)
        onward = jnp.where(odd, back.astype(jnp.float32) + side.astype(jnp.float32), back.astype(jnp.float32))
        returned = along(onward.astype(jnp.bfloat16), backward)
        mine, sink = collect(far)
        own = own + returned.astype(jnp.float32) + jnp.where(odd, 0.0, side.astype(jnp.float32))
        at = own_vertical[0] * BLK
        own = lax.dynamic_update_slice_in_dim(own, lax.dynamic_slice_in_dim(own, at, BLK, axis=1) + mine, at, axis=1)
        own = own.at[:, :BLK].add(jnp.where(seq_index == 0, sink, 0.0))
        own = own.astype(jnp.bfloat16)
        for k in range(head_size):
            piece = to_tokens(own, k, 1)
            key_pieces[k, head] = piece[0]
            value_pieces[k, head] = piece[1]
    order = [(k, head) for k in range(head_size) for head in range(kv_local)]
    return tuple(
        assemble(
            place, head_size, [query_pieces[o] for o in order], [key_pieces[o] for o in order], [value_pieces[o] for o in order]
        )
    )


def solution(mesh):
    return jax.shard_map(
        shards,
        mesh=mesh,
        in_specs=(
            P("seq", "head"),
            P("seq", "head"),
            P("seq", "head"),
            P("seq", "head"),
            P(),
            P("seq", None),
            P("seq", None),
        ),
        out_specs=(P(("seq", "head"), None), P(("seq", "head"), None), P(("seq", "head"), None)),
        check_vma=False,
    )
```

```python
import functools
import math

import jax
import jax.numpy as jnp
from jax import lax
from jax.experimental import pallas as pl
from jax.experimental.pallas import tpu as pltpu
from jax.sharding import PartitionSpec as P

HD = 128
BLK = 128
VERT_DEV = 1
FAR = 1e30


def attention_kernel(dims, place, vertical, columns, offsets, *refs):
    local_blocks, group, vert_total, heads, cuts, parts, counts = dims
    refs = list(refs)

    def take(count):
        taken = refs[:count]
        del refs[:count]
        return taken

    q_ref, do_ref, kv_own, kv_column, kv_other = take(5)
    kv_back, kv_even, kv_odd = take(counts[0]), take(counts[1]), take(counts[2])
    dq_refs, (own_ref,), prev_refs, back_refs = take(heads), take(1), take(cuts), take(cuts)
    far_refs = take(2)
    pool_k, pool_v, acc_k, acc_v, sems = refs
    turn_number = pl.program_id(0)
    seq_index, head_index = place[0], place[1]
    share = local_blocks // heads
    step = (turn_number // share ^ head_index) * share + lax.rem(turn_number, share)
    rows = local_blocks * BLK
    scale = 1.0 / math.sqrt(HD)

    @pl.when(turn_number == 0)
    def _():
        def copies(prev, parity):
            parts = [(kv_own, 0)]
            parts += [(ref, 2 * rows + at * ref.shape[1]) for at, ref in enumerate(kv_back)]
            parts += [(ref, rows + at * ref.shape[1]) for at, ref in enumerate(prev)]
            made = []
            for side, pool in enumerate((pool_k, pool_v)):
                for ref, start in parts:
                    made.append((ref.at[side], pool.at[pl.ds(start, ref.shape[1])]))
                for ref, number in ((kv_column, parity), (kv_other, 1 - parity)):
                    for plane in range(vert_total // 2):
                        into = pool.at[pl.ds(3 * rows + (2 * plane + number) * BLK, BLK)]
                        made.append((ref.at[plane, side], into))
                source = kv_other if parity else kv_column
                made.append((source.at[vert_total // 2, side], pool.at[pl.ds(3 * rows + vert_total * BLK, BLK)]))
            return [pltpu.make_async_copy(*ends, sems.at[at]) for at, ends in enumerate(made)]

        odd = lax.rem(seq_index, 2) == 1
        ways = ((odd, kv_even, 1), (jnp.logical_not(odd), kv_odd, 0))
        for way, prev, parity in ways:

            @pl.when(way)
            def _():
                for copy in copies(prev, parity):
                    copy.start()

        acc_k[...] = jnp.zeros_like(acc_k)
        acc_v[...] = jnp.zeros_like(acc_v)
        for way, prev, parity in ways:

            @pl.when(way)
            def _():
                for copy in copies(prev, parity):
                    copy.wait()

    block = seq_index * local_blocks + step

    def column_block(column):
        return column // VERT_DEV * local_blocks + vertical[column]

    def near(offset):
        at = step - offset
        return jnp.where(at >= 0, at, jnp.where(at >= -local_blocks, at + 2 * local_blocks, at + 4 * local_blocks))

    first, second = offsets[step, 0], offsets[step, 1]
    left, right = columns[step, 0], columns[step, 1]
    b2, b3 = block - first, block - second
    b4, b5 = column_block(left), column_block(right)
    far = 3 * local_blocks
    slots = [far + vert_total, step, near(first), near(second), far + left, far + right]
    live = [
        block > 0,
        None,
        b2 > 0,
        (b3 > 0) & (b3 != b2),
        (b4 > 0) & (b4 < block) & (b4 != b2) & (b4 != b3),
        (b5 > 0) & (b5 < block) & (b5 != b2) & (b5 != b3) & (b5 != b4),
    ]
    spots = [pl.ds(pl.multiple_of(slot * BLK, BLK), BLK) for slot in slots]
    queries = jnp.concatenate([q_ref[:, g * HD : (g + 1) * HD] for g in range(group)], axis=0)
    grads = jnp.concatenate([do_ref[:, g * HD : (g + 1) * HD] for g in range(group)], axis=0)
    width = group * BLK
    keys = [pool_k[spot, :] for spot in spots]
    values = [pool_v[spot, :] for spot in spots]
    contract_last = (((1,), (1,)), ((), ()))
    contract_first = (((0,), (0,)), ((), ()))
    key_at = lax.broadcasted_iota(jnp.int32, (BLK, width), 0)
    query_at = lax.broadcasted_iota(jnp.int32, (BLK, width), 1) % BLK
    seen = key_at <= query_at
    turn = scale * math.log2(math.e)
    scores, tops = [], []
    for number in range(6):
        part = lax.dot_general(keys[number], queries, contract_last, preferred_element_type=jnp.float32)
        part = part * turn
        if number == 1:
            part = jnp.where(seen, part, -FAR)
        scores.append(part)
        top = jnp.max(part, axis=0, keepdims=True)
        if number != 1:
            top = jnp.where(live[number], top, -FAR)
        tops.append(top)
    top = functools.reduce(jnp.maximum, tops)
    weights, products = [], []
    total = jnp.zeros((1, width), jnp.float32)
    delta = jnp.zeros((1, width), jnp.float32)
    for number in range(6):
        base = top if number == 1 else jnp.where(live[number], top, FAR)
        weight = jnp.exp2(scores[number] - base)
        product = lax.dot_general(values[number], grads, contract_last, preferred_element_type=jnp.float32)
        total = total + jnp.sum(weight, axis=0, keepdims=True)
        delta = delta + jnp.sum(weight * product, axis=0, keepdims=True)
        weights.append(weight)
        products.append(product)
    inverse = 1.0 / total
    delta = delta * inverse
    dq = jnp.zeros((width, HD), jnp.float32)
    for number in range(6):
        prob = weights[number] * inverse
        dscore = (prob * (products[number] - delta)).astype(jnp.bfloat16)
        prob = prob.astype(jnp.bfloat16)
        acc_v[spots[number], :] += jnp.dot(prob, grads, preferred_element_type=jnp.float32)
        acc_k[spots[number], :] += jnp.dot(dscore, queries, preferred_element_type=jnp.float32)
        dq = dq + lax.dot_general(dscore, keys[number], contract_first, preferred_element_type=jnp.float32)
    dq = (dq * scale).astype(jnp.bfloat16)
    for k, dq_ref in enumerate(dq_refs):

        @pl.when(turn_number // share == k)
        def _():
            for g in range(group):
                dq_ref[:, g * HD : (g + 1) * HD] = dq[g * BLK : (g + 1) * BLK]

    @pl.when(turn_number == local_blocks - 1)
    def _():
        size = rows // cuts // parts
        for side, (acc, factor) in enumerate(((acc_k, scale), (acc_v, 1.0))):
            for cut in range(cuts):
                for part in range(parts):
                    start = (part * cuts + cut) * size
                    into = pl.ds(part * size, size)
                    prev_refs[cut][side, into, :] = (acc[pl.ds(rows + start, size), :] * factor).astype(jnp.bfloat16)
                    back_refs[cut][side, into, :] = (acc[pl.ds(2 * rows + start, size), :] * factor).astype(jnp.bfloat16)
            own_ref[side] = acc[:rows, :] * factor

            def far_block(number):
                start = pl.multiple_of((3 * local_blocks + number) * BLK, BLK)
                return (acc[pl.ds(start, BLK), :] * factor).astype(jnp.bfloat16)

            for ref, parity in ((far_refs[0], seq_index % 2), (far_refs[1], 1 - seq_index % 2)):
                for plane in range(vert_total // 2):
                    ref[plane, side] = far_block(2 * plane + parity)
                ref[vert_total // 2, side] = far_block(vert_total)


def attention(
    head, kv_local, heads, cuts, parts, place, vertical, columns, offsets, queries, grad_out, kv_own, kv_column, kv_other,
    kv_back, kv_even, kv_odd
):
    seq_len = queries.shape[0]
    local_blocks = seq_len // BLK
    width = queries.shape[1] // kv_local
    group = width // HD
    vert_total = vertical.shape[0]
    total_rows = 3 * seq_len + (vert_total + 1) * BLK
    anywhere = pl.BlockSpec(memory_space=pl.ANY)
    share = local_blocks // heads
    by_block = pl.BlockSpec((BLK, width), lambda i, place, *_: ((i // share ^ place[1]) * share + i % share, head))

    def whole(*shape):
        return pl.BlockSpec(shape, lambda i, *_: (0,) * len(shape))

    def share_spec(k):
        return pl.BlockSpec((BLK, width), lambda i, *_: (jnp.clip(i - k * share, 0, share - 1), 0))

    near_shape = (2, seq_len, HD)
    cut_shape = (2, seq_len // cuts, HD)
    block_shape = (2, BLK, HD)
    far_shapes = [(vert_total // 2 + 1, *block_shape)] * 2
    flops = 2 * 5 * seq_len * group * 6 * BLK * HD
    pools = [*kv_back, *kv_even, *kv_odd]
    counts = (len(kv_back), len(kv_even), len(kv_odd))
    outs = pl.pallas_call(
        functools.partial(attention_kernel, (local_blocks, group, vert_total, heads, cuts, parts, counts)),
        grid_spec=pltpu.PrefetchScalarGridSpec(
            num_scalar_prefetch=4,
            grid=(local_blocks,),
            in_specs=[by_block, by_block] + [anywhere] * (3 + len(pools)),
            out_specs=[share_spec(k) for k in range(heads)]
            + [whole(*near_shape)]
            + [whole(*cut_shape)] * (2 * cuts)
            + [whole(*shape) for shape in far_shapes],
            scratch_shapes=[
                pltpu.VMEM((total_rows, HD), jnp.bfloat16),
                pltpu.VMEM((total_rows, HD), jnp.bfloat16),
                pltpu.VMEM((total_rows, HD), jnp.float32),
                pltpu.VMEM((total_rows, HD), jnp.float32),
                pltpu.SemaphoreType.DMA((2 * (2 + len(pools) + vert_total),)),
            ],
        ),
        out_shape=[jax.ShapeDtypeStruct((seq_len // heads, width), jnp.bfloat16)] * heads
        + [jax.ShapeDtypeStruct(near_shape, jnp.float32)]
        + [jax.ShapeDtypeStruct(cut_shape, jnp.bfloat16)] * (2 * cuts)
        + [jax.ShapeDtypeStruct(shape, jnp.bfloat16) for shape in far_shapes],
        compiler_params=pltpu.CompilerParams(vmem_limit_bytes=50 * 1024 * 1024),
        cost_estimate=pl.CostEstimate(
            flops=4 * flops, bytes_accessed=20 * 1024 * 1024, transcendentals=seq_len * group * 6 * BLK
        ),
        name="attention",
    )(place, vertical, columns, offsets, queries, grad_out, kv_own, kv_column, kv_other, *pools)
    at = heads + 1
    return outs[:heads], outs[heads], outs[at : at + cuts], outs[at + cuts : at + 2 * cuts], *outs[at + 2 * cuts :]


def queries_kernel(heads, kv_local, place, *refs):
    for k in range(heads):
        for head in range(kv_local):
            piece = refs[k * kv_local + head]
            width = piece.shape[1]
            column = (place[1] ^ k) * kv_local + head
            refs[-1][:, pl.ds(pl.multiple_of(column * width, width), width)] = piece[...]


def assemble_queries(place, heads, kv_local, pieces):
    rows, width = pieces[0, 0].shape
    tile = min(rows, 128)
    count = heads * kv_local
    return pl.pallas_call(
        functools.partial(queries_kernel, heads, kv_local),
        grid_spec=pltpu.PrefetchScalarGridSpec(
            num_scalar_prefetch=1,
            grid=(rows // tile,),
            in_specs=[pl.BlockSpec((tile, width), lambda i, *_: (i, 0))] * count,
            out_specs=pl.BlockSpec((tile, width * count), lambda i, *_: (i, 0)),
        ),
        out_shape=jax.ShapeDtypeStruct((rows, width * count), jnp.bfloat16),
        name="assemble_queries",
    )(place, *(pieces[k, head] for k in range(heads) for head in range(kv_local)))


def pairs_kernel(heads, kv_local, cuts, place, *refs):
    k_out, v_out = refs[-2:]
    refs = list(refs[:-2])
    for k in range(heads):
        for head in range(kv_local):
            column = (place[1] ^ k) * kv_local + head
            spot = pl.ds(pl.multiple_of(column * HD, HD), HD)
            for cut in range(cuts[head]):
                both = refs.pop(0)
                size = both.shape[1]
                k_out[pl.ds(cut * size, size), spot] = both[0]
                v_out[pl.ds(cut * size, size), spot] = both[1]


def assemble_pairs(place, heads, kv_local, cuts, pieces):
    arrays = [pieces[k, head, cut] for k in range(heads) for head in range(kv_local) for cut in range(cuts[head])]
    rows = pieces[0, 0, 0].shape[1] * cuts[0]
    out_shape = jax.ShapeDtypeStruct((rows, HD * heads * kv_local), jnp.bfloat16)
    return pl.pallas_call(
        functools.partial(pairs_kernel, heads, kv_local, cuts),
        grid_spec=pltpu.PrefetchScalarGridSpec(
            num_scalar_prefetch=1,
            grid=(1,),
            in_specs=[pl.BlockSpec(array.shape, lambda i, *_: (0, 0, 0)) for array in arrays],
            out_specs=[pl.BlockSpec(out_shape.shape, lambda i, *_: (0, 0))] * 2,
        ),
        out_shape=[out_shape] * 2,
        name="assemble_pairs",
    )(place, *arrays)


def after(value, *others):
    return lax.optimization_barrier((value, others))[0]


def shards(queries, keys, values, grad_out, vertical, columns, offsets):
    seq_len = queries.shape[0]
    seq_size = lax.axis_size("seq")
    heads = lax.axis_size("head")
    kv_local = keys.shape[1] // HD
    local_blocks = seq_len // BLK
    cuts = 2
    half = seq_len // 2
    seq_index = lax.axis_index("seq")
    head_index = lax.axis_index("head")
    place = jnp.stack([seq_index, head_index]).astype(jnp.int32)
    odd = seq_index % 2 == 1
    levels = [1 << level for level in range(int(math.log2(seq_size)))]

    def along(array, pairs, name):
        with jax.named_scope(name):
            return lax.ppermute(array, "seq", pairs)

    def across(array, k, name):
        with jax.named_scope(name):
            return lax.ppermute(array, "head", [(i, i ^ k) for i in range(heads)]) if k else array

    def shift(by, only=None):
        return [(i, i + by) for i in range(seq_size) if 0 <= i + by < seq_size and only in (None, i % 2)]

    exchange = [(i, i ^ 1) for i in range(seq_size)]
    own_vertical = lax.dynamic_slice_in_dim(vertical, seq_index * VERT_DEV, VERT_DEV)[0]
    kvs = [
        jnp.stack([keys[:, head * HD : (head + 1) * HD], values[:, head * HD : (head + 1) * HD]])
        for head in range(kv_local)
    ]
    mine = jnp.stack([lax.dynamic_slice_in_dim(kv, own_vertical * BLK, BLK, axis=1) for kv in kvs])
    sink = jnp.stack([kv[:, :BLK] for kv in kvs])
    groups = [list(range(0, seq_size, 2)), list(range(1, seq_size, 2))]

    def column_of(block, name):
        with jax.named_scope(name):
            wide = jnp.broadcast_to(block, (seq_size // 2, *block.shape))
            return lax.all_to_all(wide, "seq", split_axis=0, concat_axis=0, axis_index_groups=groups)

    first = sink
    for hop in reversed(levels[1:]):
        got = along(first, [(i, i + hop) for i in range(0, seq_size, 2 * hop)], f"in_first{hop}")
        first = jnp.where(seq_index % (2 * hop) == hop, got, first)

    fetched = []
    for head, kv in enumerate(kvs):
        block = mine[head]
        if head:
            kv, block = after((kv, block), fetched[0][1][1])
        backs = [along(kv[:, :half], shift(2), f"in_back{head}_a")]
        kv_column = jnp.concatenate([column_of(block, f"in_column{head}"), first[None, head]])
        kv_other = along(kv_column, exchange, f"in_column_pair{head}")
        if head:
            backs.append(along(after(kv[:, half:], backs[0]), shift(2), f"in_back{head}_b"))
            odds = [along(backs[0], shift(-1, 1), f"in_odd{head}_a"), along(after(kv[:, half:], backs[0]), shift(1, 1), f"in_odd{head}_b")]
        else:
            backs.append(along(after(kv[:, half:], backs[0]), shift(2), f"in_back{head}_b"))
            odds = [along(backs[0], shift(-1, 1), f"in_odd{head}_a"), along(after(backs[1], kv_other), shift(-1, 1), f"in_odd{head}_b")]
        evens = [along(kv, shift(1, 0), f"in_even{head}")]
        fetched.append((kv, backs, evens, odds, kv_column, kv_other))
    if kv_local > 1:
        place = after(place, fetched[1][1][0], fetched[1][4])

    query_pieces, pair_pieces, results, far_pairs = {}, {}, [], []
    planes = seq_size // 2
    cut_counts = [cuts if head + 1 == kv_local else 1 for head in range(kv_local)]
    for head, (kv, backs, evens, odds, kv_column, kv_other) in enumerate(fetched):
        last = head + 1 == kv_local
        dqs, own, prevs, backs, *fars = attention(
            head, kv_local, heads, cut_counts[head], heads if last else 1,
            place, vertical, columns, offsets, queries, grad_out, kv, kv_column, kv_other, backs, evens, odds,
        )
        if not last:
            far_pairs.append((fars[0], along(fars[1], exchange, f"out_far_pair{head}")))
            for k in range(heads):
                query_pieces[k, head] = across(dqs[k], k, f"out_query{head}_{k}")
            sides = [along(prev, exchange, f"out_pair{head}") for prev in prevs]
            results.append((own, sides, backs))
            continue
        if head:
            results = after(results, dqs[0])
            before = [query_pieces[k, head - 1] for k in range(heads)]
            prevs, fars, dqs = after((prevs, fars, dqs), before, far_pairs, results)
        first_k = heads // 2
        sides = [along(prevs[0], exchange, f"out_pair{head}_0")]
        far_pairs.append((fars[0], along(fars[1], exchange, f"out_far_pair{head}")))
        query_pieces[first_k, head] = across(dqs[first_k], first_k, f"out_query{head}_{first_k}")

        def onward(back, side, name):
            total = back.astype(jnp.float32) + jnp.where(odd, side.astype(jnp.float32), 0.0)
            return along(total.astype(jnp.bfloat16), shift(-2), name)

        for at, (own_before, sides_before, backs_before) in enumerate(results):
            returned = [onward(back, side, f"out_onward{at}") for back, side in zip(backs_before, sides_before)]
            results[at] = (own_before, sides_before, returned)
        far_sum = jnp.stack([keep.astype(jnp.float32) + pair.astype(jnp.float32) for keep, pair in far_pairs], axis=1)
        first = far_sum[planes]
        with jax.named_scope("out_far"):
            far = lax.all_to_all(
                far_sum[:planes].astype(jnp.bfloat16), "seq", split_axis=0, concat_axis=0, axis_index_groups=groups
            )
        far = jnp.sum(far.astype(jnp.float32), axis=0)
        prevs, dqs = after((prevs, dqs), far_sum, query_pieces[first_k, head])
        sides += [along(prev, exchange, f"out_pair{head}_{cut + 1}") for cut, prev in enumerate(prevs[1:])]
        for hop in levels[1:]:
            pairs = [(i + hop, i) for i in range(0, seq_size, 2 * hop)]
            first = first + along(first.astype(jnp.bfloat16), pairs, f"out_first{hop}").astype(jnp.float32)
        for k in range(heads):
            if k != first_k:
                query_pieces[k, head] = across(dqs[k], k, f"out_query{head}_{k}")
        sides[1] = after(sides[1], [query_pieces[k, head] for k in range(heads)])
        returned = [onward(back, side, f"out_onward{head}_{cut}") for cut, (back, side) in enumerate(zip(backs, sides))]
        results.append((own, sides, returned))

    def token_blocks(array, parts):
        return array.reshape(2, heads, parts, -1, BLK, HD).astype(jnp.float32)

    for head, (own, sides, returned) in enumerate(results):
        count = cut_counts[head]
        if head + 1 == kv_local:
            returned = after(returned, list(pair_pieces.values()))
            query_out = assemble_queries(place, heads, kv_local, query_pieces)
        block_ids = jnp.arange(local_blocks).reshape(1, heads, count, -1, 1, 1)
        for cut in range(count):
            if cut:
                returned = after(returned, query_out, [pair_pieces[k, head, cut - 1] for k in range(heads)])
            total = token_blocks(own, count)[:, :, cut : cut + 1]
            side = token_blocks(sides[cut], 1)
            total = total + jnp.where(odd, 0.0, side) + token_blocks(returned[cut], 1)
            block = block_ids[:, :, cut : cut + 1]
            total = total + jnp.where(block == own_vertical, far[head][:, None, None, None], 0.0)
            total = total + jnp.where((block == 0) & (seq_index == 0), first[head][:, None, None, None], 0.0)
            total = total.astype(jnp.bfloat16).reshape(2, heads, -1, HD)
            for k in range(heads):
                piece = lax.dynamic_index_in_dim(total, head_index ^ k, 1, keepdims=False)
                pair_pieces[k, head, cut] = across(piece, k, f"out_pairs{head}_{cut}_{k}")
    return (query_out, *assemble_pairs(place, heads, kv_local, cut_counts, pair_pieces))


def solution(mesh):
    return jax.shard_map(
        shards,
        mesh=mesh,
        in_specs=(
            P("seq", "head"),
            P("seq", "head"),
            P("seq", "head"),
            P("seq", "head"),
            P(),
            P("seq", None),
            P("seq", None),
        ),
        out_specs=(P(("seq", "head"), None), P(("seq", "head"), None), P(("seq", "head"), None)),
        check_vma=False,
    )
```

```python
import functools
import math

import jax
import jax.numpy as jnp
from jax import lax
from jax.experimental import pallas as pl
from jax.experimental.pallas import tpu as pltpu
from jax.sharding import PartitionSpec as P

HD = 128
BLK = 128
VERT_DEV = 1
FAR = 1e30


def attention_kernel(dims, place, vertical, columns, offsets, *refs):
    local_blocks, group, vert_total, heads, last = dims
    refs = list(refs)

    def take(count):
        taken = refs[:count]
        del refs[:count]
        return taken

    q_ref, do_ref, kv_own, kv_column, kv_other = take(5)
    kv_back, kv_even, kv_odd = take(3)
    dq_refs, (own_ref, prev_ref, back_ref), far_refs = take(heads), take(3), take(2 if last else 1)
    pool_k, pool_v, acc_k, acc_v, dq_out, sems = refs
    turn_number = pl.program_id(0)
    seq_index, head_index = place[0], place[1]
    share = local_blocks // heads
    together = min(4, share)
    turns = share // together
    step_base = ((turn_number // turns ^ head_index) * turns + lax.rem(turn_number, turns)) * together
    rows = local_blocks * BLK
    scale = 1.0 / math.sqrt(HD)

    @pl.when(turn_number == 0)
    def _():
        def copies(prev, parity):
            parts = [(kv_own, 0), (prev, rows), (kv_back, 2 * rows)]
            made = []
            for side, pool in enumerate((pool_k, pool_v)):
                for ref, start in parts:
                    made.append((ref.at[side], pool.at[pl.ds(start, ref.shape[1])]))
                for ref, number in ((kv_column, parity), (kv_other, 1 - parity)):
                    for plane in range(vert_total // 2):
                        into = pool.at[pl.ds(3 * rows + (2 * plane + number) * BLK, BLK)]
                        made.append((ref.at[plane, side], into))
                source = kv_other if parity else kv_column
                made.append((source.at[vert_total // 2, side], pool.at[pl.ds(3 * rows + vert_total * BLK, BLK)]))
            return [pltpu.make_async_copy(*ends, sems.at[at]) for at, ends in enumerate(made)]

        odd = lax.rem(seq_index, 2) == 1
        ways = ((odd, kv_even, 1), (jnp.logical_not(odd), kv_odd, 0))
        for way, prev, parity in ways:

            @pl.when(way)
            def _():
                for copy in copies(prev, parity):
                    copy.start()

        acc_k[...] = jnp.zeros_like(acc_k)
        acc_v[...] = jnp.zeros_like(acc_v)
        for way, prev, parity in ways:

            @pl.when(way)
            def _():
                for copy in copies(prev, parity):
                    copy.wait()

    scale_two = scale * math.log2(math.e)
    contract_last = (((1,), (1,)), ((), ()))
    contract_first = (((0,), (0,)), ((), ()))
    width = group * BLK
    seen = lax.broadcasted_iota(jnp.int32, (BLK, width), 0) <= lax.broadcasted_iota(jnp.int32, (BLK, width), 1) % BLK

    def column_block(column):
        return column // VERT_DEV * local_blocks + vertical[column]

    def stacked(ref, here):
        return jnp.concatenate([ref[here, g * HD : (g + 1) * HD] for g in range(group)], axis=0)

    def begin(sub):
        step = step_base + sub
        block = seq_index * local_blocks + step
        here = slice(sub * BLK, (sub + 1) * BLK)

        def near(offset):
            at = step - offset
            return jnp.where(at >= 0, at, jnp.where(at >= -local_blocks, at + 2 * local_blocks, at + 4 * local_blocks))

        first, second = offsets[step, 0], offsets[step, 1]
        left, right = columns[step, 0], columns[step, 1]
        b2, b3 = block - first, block - second
        b4, b5 = column_block(left), column_block(right)
        far = 3 * local_blocks
        slots = [far + vert_total, step, near(first), near(second), far + left, far + right]
        live = [
            block > 0,
            None,
            b2 > 0,
            (b3 > 0) & (b3 != b2),
            (b4 > 0) & (b4 < block) & (b4 != b2) & (b4 != b3),
            (b5 > 0) & (b5 < block) & (b5 != b2) & (b5 != b3) & (b5 != b4),
        ]
        spots = [pl.ds(pl.multiple_of(slot * BLK, BLK), BLK) for slot in slots]
        queries, grads = stacked(q_ref, here), stacked(do_ref, here)
        keys = jnp.concatenate([pool_k[spot, :] for spot in spots], axis=0)
        values = jnp.concatenate([pool_v[spot, :] for spot in spots], axis=0)
        score = lax.dot_general(keys, queries, contract_last, preferred_element_type=jnp.float32)
        product = lax.dot_general(values, grads, contract_last, preferred_element_type=jnp.float32)
        return live, spots, queries, grads, keys, score, product

    def weigh(live, score, product):
        scores, tops, weights, probs, dscores = [], [], [], [], []
        for number in range(6):
            part = score[number * BLK : (number + 1) * BLK] * scale_two
            if number == 1:
                part = jnp.where(seen, part, -FAR)
            scores.append(part)
            top = jnp.max(part, axis=0, keepdims=True)
            tops.append(top if number == 1 else jnp.where(live[number], top, -FAR))
        top = functools.reduce(jnp.maximum, tops)
        total, delta = 0.0, 0.0
        for number in range(6):
            weight = jnp.exp2(scores[number] - (top if number == 1 else jnp.where(live[number], top, FAR)))
            total = total + jnp.sum(weight, axis=0, keepdims=True)
            delta = delta + jnp.sum(weight * product[number * BLK : (number + 1) * BLK], axis=0, keepdims=True)
            weights.append(weight)
        inverse = 1.0 / total
        delta = delta * inverse
        for number in range(6):
            prob = weights[number] * inverse
            dscores.append((prob * (product[number * BLK : (number + 1) * BLK] - delta)).astype(jnp.bfloat16))
            probs.append(prob.astype(jnp.bfloat16))
        return jnp.concatenate(probs, axis=0), jnp.concatenate(dscores, axis=0)

    def finish(sub, spots, queries, grads, keys, prob, dscore):
        value_terms = jnp.dot(prob, grads, preferred_element_type=jnp.float32)
        key_terms = jnp.dot(dscore, queries, preferred_element_type=jnp.float32)
        dq = lax.dot_general(dscore, keys, contract_first, preferred_element_type=jnp.float32)
        dq = (dq * scale).astype(jnp.bfloat16)
        for number, spot in enumerate(spots):
            acc_v[spot, :] += value_terms[number * BLK : (number + 1) * BLK]
            acc_k[spot, :] += key_terms[number * BLK : (number + 1) * BLK]
        for g in range(group):
            dq_out[sub * BLK : (sub + 1) * BLK, g * HD : (g + 1) * HD] = dq[g * BLK : (g + 1) * BLK]

    begun = begin(0)
    for sub in range(together):
        live, spots, queries, grads, keys, score, product = begun
        if sub + 1 < together:
            begun = begin(sub + 1)
        prob, dscore = weigh(live, score, product)
        finish(sub, spots, queries, grads, keys, prob, dscore)

    for k, dq_ref in enumerate(dq_refs):

        @pl.when(turn_number // (share // together) == k)
        def _():
            dq_ref[...] = dq_out[...]

    @pl.when(turn_number == local_blocks // together - 1)
    def _():
        for side, (acc, factor) in enumerate(((acc_k, scale), (acc_v, 1.0))):
            prev_ref[side] = (acc[rows : 2 * rows, :] * factor).astype(jnp.bfloat16)
            back_ref[side] = (acc[2 * rows : 3 * rows, :] * factor).astype(jnp.bfloat16)
            own_ref[side] = acc[:rows, :] * factor

            def far_block(number):
                start = pl.multiple_of((3 * local_blocks + number) * BLK, BLK)
                return (acc[pl.ds(start, BLK), :] * factor).astype(jnp.bfloat16)

            if last:
                for ref, parity in ((far_refs[0], seq_index % 2), (far_refs[1], 1 - seq_index % 2)):
                    for plane in range(vert_total // 2):
                        ref[plane, side] = far_block(2 * plane + parity)
                    ref[vert_total // 2, side] = far_block(vert_total)
            else:
                sink = far_block(vert_total)
                for number in range(vert_total):
                    far_refs[0][number, 0, side] = far_block(number)
                    far_refs[0][number, 1, side] = sink


def attention(
    head, kv_local, heads, place, vertical, columns, offsets, queries, grad_out, kv_own, kv_column, kv_other,
    kv_back, kv_even, kv_odd
):
    seq_len = queries.shape[0]
    local_blocks = seq_len // BLK
    width = queries.shape[1] // kv_local
    group = width // HD
    vert_total = vertical.shape[0]
    total_rows = 3 * seq_len + (vert_total + 1) * BLK
    anywhere = pl.BlockSpec(memory_space=pl.ANY)
    share = local_blocks // heads
    together = min(4, share)
    turns = share // together
    by_block = pl.BlockSpec((together * BLK, width), lambda i, place, *_: ((i // turns ^ place[1]) * turns + i % turns, head))

    def whole(*shape):
        return pl.BlockSpec(shape, lambda i, *_: (0,) * len(shape))

    def share_spec(k):
        return pl.BlockSpec((together * BLK, width), lambda i, *_: (jnp.clip(i - k * turns, 0, turns - 1), 0))

    near_shape = (2, seq_len, HD)
    block_shape = (2, BLK, HD)
    last = head + 1 == kv_local
    far_shapes = [(vert_total // 2 + 1, *block_shape)] * 2 if last else [(vert_total, 2, *block_shape)]
    flops = 2 * 5 * seq_len * group * 6 * BLK * HD
    outs = pl.pallas_call(
        functools.partial(attention_kernel, (local_blocks, group, vert_total, heads, last)),
        grid_spec=pltpu.PrefetchScalarGridSpec(
            num_scalar_prefetch=4,
            grid=(local_blocks // together,),
            in_specs=[by_block, by_block] + [anywhere] * 6,
            out_specs=[share_spec(k) for k in range(heads)]
            + [whole(*near_shape)] * 3
            + [whole(*shape) for shape in far_shapes],
            scratch_shapes=[
                pltpu.VMEM((total_rows, HD), jnp.bfloat16),
                pltpu.VMEM((total_rows, HD), jnp.bfloat16),
                pltpu.VMEM((total_rows, HD), jnp.float32),
                pltpu.VMEM((total_rows, HD), jnp.float32),
                pltpu.VMEM((together * BLK, width), jnp.bfloat16),
                pltpu.SemaphoreType.DMA((2 * (4 + vert_total),)),
            ],
        ),
        out_shape=[jax.ShapeDtypeStruct((seq_len // heads, width), jnp.bfloat16)] * heads
        + [jax.ShapeDtypeStruct(near_shape, jnp.float32)]
        + [jax.ShapeDtypeStruct(near_shape, jnp.bfloat16)] * 2
        + [jax.ShapeDtypeStruct(shape, jnp.bfloat16) for shape in far_shapes],
        compiler_params=pltpu.CompilerParams(vmem_limit_bytes=50 * 1024 * 1024),
        cost_estimate=pl.CostEstimate(
            flops=4 * flops, bytes_accessed=20 * 1024 * 1024, transcendentals=seq_len * group * 6 * BLK
        ),
        name="attention",
    )(place, vertical, columns, offsets, queries, grad_out, kv_own, kv_column, kv_other, kv_back, kv_even, kv_odd)
    return outs[:heads], *outs[heads:]


def queries_kernel(heads, kv_local, place, *refs):
    for k in range(heads):
        for head in range(kv_local):
            piece = refs[k * kv_local + head]
            width = piece.shape[1]
            column = (place[1] ^ k) * kv_local + head
            refs[-1][:, pl.ds(pl.multiple_of(column * width, width), width)] = piece[...]


def assemble_queries(place, heads, kv_local, pieces):
    rows, width = pieces[0, 0].shape
    tile = min(rows, 128)
    count = heads * kv_local
    return pl.pallas_call(
        functools.partial(queries_kernel, heads, kv_local),
        grid_spec=pltpu.PrefetchScalarGridSpec(
            num_scalar_prefetch=1,
            grid=(rows // tile,),
            in_specs=[pl.BlockSpec((tile, width), lambda i, *_: (i, 0))] * count,
            out_specs=pl.BlockSpec((tile, width * count), lambda i, *_: (i, 0)),
        ),
        out_shape=jax.ShapeDtypeStruct((rows, width * count), jnp.bfloat16),
        name="assemble_queries",
    )(place, *(pieces[k, head] for k in range(heads) for head in range(kv_local)))


def pairs_kernel(heads, kv_local, place, *refs):
    k_out, v_out = refs[-2:]
    for k in range(heads):
        for head in range(kv_local):
            column = (place[1] ^ k) * kv_local + head
            spot = pl.ds(pl.multiple_of(column * HD, HD), HD)
            both = refs[k * kv_local + head]
            k_out[:, spot] = both[0]
            v_out[:, spot] = both[1]


def assemble_pairs(place, heads, kv_local, pieces):
    arrays = [pieces[k, head] for k in range(heads) for head in range(kv_local)]
    rows = arrays[0].shape[1]
    tile = min(rows, 256)
    out_shape = jax.ShapeDtypeStruct((rows, HD * heads * kv_local), jnp.bfloat16)
    return pl.pallas_call(
        functools.partial(pairs_kernel, heads, kv_local),
        grid_spec=pltpu.PrefetchScalarGridSpec(
            num_scalar_prefetch=1,
            grid=(rows // tile,),
            in_specs=[pl.BlockSpec((2, tile, HD), lambda i, *_: (0, i, 0))] * len(arrays),
            out_specs=[pl.BlockSpec((tile, out_shape.shape[1]), lambda i, *_: (i, 0))] * 2,
        ),
        out_shape=[out_shape] * 2,
        name="assemble_pairs",
    )(place, *arrays)


def after(value, *others):
    return lax.optimization_barrier((value, others))[0]


def shards(queries, keys, values, grad_out, vertical, columns, offsets):
    seq_len = queries.shape[0]
    seq_size = lax.axis_size("seq")
    heads = lax.axis_size("head")
    kv_local = keys.shape[1] // HD
    local_blocks = seq_len // BLK
    seq_index = lax.axis_index("seq")
    head_index = lax.axis_index("head")
    place = jnp.stack([seq_index, head_index]).astype(jnp.int32)
    odd = seq_index % 2 == 1
    levels = [1 << level for level in range(int(math.log2(seq_size)))]

    def along(array, pairs, name):
        with jax.named_scope(name):
            return lax.ppermute(array, "seq", pairs)

    def across(array, k, name):
        with jax.named_scope(name):
            return lax.ppermute(array, "head", [(i, i ^ k) for i in range(heads)]) if k else array

    def shift(by, only=None):
        return [(i, i + by) for i in range(seq_size) if 0 <= i + by < seq_size and only in (None, i % 2)]

    exchange = [(i, i ^ 1) for i in range(seq_size)]
    own_vertical = lax.dynamic_slice_in_dim(vertical, seq_index * VERT_DEV, VERT_DEV)[0]
    kvs = [
        jnp.stack([keys[:, head * HD : (head + 1) * HD], values[:, head * HD : (head + 1) * HD]])
        for head in range(kv_local)
    ]
    mine = jnp.stack([lax.dynamic_slice_in_dim(kv, own_vertical * BLK, BLK, axis=1) for kv in kvs])
    sink = jnp.stack([kv[:, :BLK] for kv in kvs])
    groups = [list(range(0, seq_size, 2)), list(range(1, seq_size, 2))]

    def column_of(block, name):
        with jax.named_scope(name):
            wide = jnp.broadcast_to(block, (seq_size // 2, *block.shape))
            return lax.all_to_all(wide, "seq", split_axis=0, concat_axis=0, axis_index_groups=groups)

    first = sink
    for hop in reversed(levels[1:]):
        got = along(first, [(i, i + hop) for i in range(0, seq_size, 2 * hop)], f"in_first{hop}")
        first = jnp.where(seq_index % (2 * hop) == hop, got, first)

    column = column_of(mine, "in_column")
    kv_columns = [jnp.concatenate([column[:, head], first[None, head]]) for head in range(kv_local)]

    fetched = []
    for head, kv in enumerate(kvs):
        kv_column = kv_columns[head]
        if head:
            kv, kv_column = after((kv, kv_column), fetched[-1][1], fetched[-1][5])
        kv_other = along(kv_column, exchange, f"in_column_pair{head}")
        if head:
            back, even = along(kv, shift(2), f"in_back{head}"), along(kv, shift(1), f"in_prev{head}")
            odd_prev = even
        else:
            back, even = along(kv, shift(2), f"in_back{head}"), along(kv, shift(1, 0), f"in_even{head}")
            odd_prev = along(after(back, kv_other), shift(-1, 1), f"in_odd{head}")
        fetched.append((kv, back, even, odd_prev, kv_column, kv_other))

    planes = seq_size // 2
    query_pieces, pair_pieces, results, fars = {}, {}, [], []

    def onward(back, side):
        return (back.astype(jnp.float32) + jnp.where(odd, side.astype(jnp.float32), 0.0)).astype(jnp.bfloat16)

    for head, (kv, back, even, odd_prev, kv_column, kv_other) in enumerate(fetched):
        last = head + 1 == kv_local
        dqs, own, prev, back, *table = attention(
            head, kv_local, heads, place, vertical, columns, offsets, queries, grad_out, kv, kv_column, kv_other, back, even, odd_prev
        )
        if not last:
            with jax.named_scope(f"out_far{head}"):
                fars.append(lax.all_to_all(table[0], "seq", split_axis=0, concat_axis=0))
            for k in range(heads):
                query_pieces[k, head] = across(dqs[k], k, f"out_query{head}_{k}")
            results.append((own, along(prev, exchange, f"out_pair{head}"), back))
            continue
        keep, give = table
        if head:
            before = [query_pieces[k, head - 1] for k in range(heads)]
            fars, results = after((fars, results), dqs[0])
            prev, give, dqs = after((prev, give, dqs), before, fars, results)
        got = along(give, exchange, f"out_far_pair{head}")
        for k in range(2, heads):
            query_pieces[k, head] = across(dqs[k], k, f"out_query{head}_{k}")
        sent = [onward(back_before, side_before) for _, side_before, back_before in results]
        side = along(after(prev, sent), exchange, f"out_pair{head}")
        results = [
            (own_before, side_before, along(piece, shift(-2), f"out_onward{at}"))
            for at, ((own_before, side_before, _), piece) in enumerate(zip(results, sent))
        ]
        far_sum = (keep.astype(jnp.float32) + got.astype(jnp.float32)).astype(jnp.bfloat16)
        far_sum = jnp.stack([far_sum[:planes], jnp.broadcast_to(far_sum[planes], far_sum[:planes].shape)], axis=1)
        with jax.named_scope("out_far"):
            fars.append(lax.all_to_all(far_sum, "seq", split_axis=0, concat_axis=0, axis_index_groups=groups))
        fars = [jnp.sum(terms.astype(jnp.float32), axis=0) for terms in fars]
        if heads > 1:
            query_pieces[1, head] = across(after(dqs[1], far_sum), 1, f"out_query{head}_1")
        query_pieces[0, head] = dqs[0]
        results.append((own, side, along(onward(back, side), shift(-2), f"out_onward{head}")))

    block_ids = jnp.arange(local_blocks)[None, :, None, None]
    for head, (own, side, returned) in enumerate(results):
        if head and head + 1 == kv_local:
            query_out = assemble_queries(place, heads, kv_local, query_pieces)
            returned = after(returned, query_out, list(pair_pieces.values()))
        elif kv_local == 1:
            query_out = assemble_queries(place, heads, kv_local, query_pieces)

        def blocked(array):
            return array.reshape(2, local_blocks, BLK, HD).astype(jnp.float32)

        total = blocked(own) + (jnp.where(odd, 0.0, blocked(side)) + blocked(returned))
        total = total + jnp.where(block_ids == own_vertical, fars[head][0][:, None], 0.0)
        total = total + jnp.where((block_ids == 0) & (seq_index == 0), fars[head][1][:, None], 0.0)
        total = total.astype(jnp.bfloat16).reshape(2, heads, -1, HD)
        for k in range(heads):
            piece = lax.dynamic_index_in_dim(total, head_index ^ k, 1, keepdims=False)
            pair_pieces[k, head] = across(piece, k, f"out_pairs{head}_{k}")
    return (query_out, *assemble_pairs(place, heads, kv_local, pair_pieces))


def solution(mesh):
    return jax.shard_map(
        shards,
        mesh=mesh,
        in_specs=(
            P("seq", "head"),
            P("seq", "head"),
            P("seq", "head"),
            P("seq", "head"),
            P(),
            P("seq", None),
            P("seq", None),
        ),
        out_specs=(P(("seq", "head"), None), P(("seq", "head"), None), P(("seq", "head"), None)),
        check_vma=False,
    )
```

```python
import functools
import math

import jax
import jax.numpy as jnp
from jax import lax
from jax.experimental import pallas as pl
from jax.experimental.pallas import tpu as pltpu
from jax.sharding import PartitionSpec as P

HD = 128
BLK = 128
VERT_DEV = 1
FAR = 1e30


def attention_kernel(dims, place, vertical, columns, offsets, *refs):
    local_blocks, group, vert_total, heads, head, last = dims
    refs = list(refs)

    def take(count):
        taken = refs[:count]
        del refs[:count]
        return taken

    q_ref, do_ref, kv_own, kv_column, kv_other, first_even, first_odd = take(7)
    kv_back, kv_even, kv_odd = take(3)
    dq_refs, (own_ref, prev_ref, back_ref), far_refs = take(heads), take(3), take(2 if last else 1)
    pool_k, pool_v, acc_k, acc_v, dq_out, sems = refs
    turn_number = pl.program_id(0)
    seq_index, head_index = place[0], place[1]
    share = local_blocks // heads
    together = min(4, share)
    turns = share // together
    step_base = ((turn_number // turns ^ head_index) * turns + lax.rem(turn_number, turns)) * together
    rows = local_blocks * BLK
    scale = 1.0 / math.sqrt(HD)

    @pl.when(turn_number == 0)
    def _():
        def copies(prev, parity):
            parts = [(kv_own, 0), (prev, rows), (kv_back, 2 * rows)]
            made = []
            for side, pool in enumerate((pool_k, pool_v)):
                for ref, start in parts:
                    made.append((ref.at[side], pool.at[pl.ds(start, ref.shape[1])]))
                for ref, number in ((kv_column, parity), (kv_other, 1 - parity)):
                    for plane in range(vert_total // 2):
                        into = pool.at[pl.ds(3 * rows + (2 * plane + number) * BLK, BLK)]
                        made.append((ref.at[plane, side], into))
                source = first_odd if parity else first_even
                made.append((source.at[head, side], pool.at[pl.ds(3 * rows + vert_total * BLK, BLK)]))
            return [pltpu.make_async_copy(*ends, sems.at[at]) for at, ends in enumerate(made)]

        odd = lax.rem(seq_index, 2) == 1
        ways = ((odd, kv_even, 1), (jnp.logical_not(odd), kv_odd, 0))
        for way, prev, parity in ways:

            @pl.when(way)
            def _():
                for copy in copies(prev, parity):
                    copy.start()

        acc_k[...] = jnp.zeros_like(acc_k)
        acc_v[...] = jnp.zeros_like(acc_v)
        for way, prev, parity in ways:

            @pl.when(way)
            def _():
                for copy in copies(prev, parity):
                    copy.wait()

    scale_two = scale * math.log2(math.e)
    contract_last = (((1,), (1,)), ((), ()))
    contract_first = (((0,), (0,)), ((), ()))
    width = group * BLK
    seen = lax.broadcasted_iota(jnp.int32, (BLK, width), 0) <= lax.broadcasted_iota(jnp.int32, (BLK, width), 1) % BLK

    def column_block(column):
        return column // VERT_DEV * local_blocks + vertical[column]

    def stacked(ref, here):
        return jnp.concatenate([ref[here, g * HD : (g + 1) * HD] for g in range(group)], axis=0)

    def begin(sub):
        step = step_base + sub
        block = seq_index * local_blocks + step
        here = slice(sub * BLK, (sub + 1) * BLK)

        def near(offset):
            at = step - offset
            return jnp.where(at >= 0, at, jnp.where(at >= -local_blocks, at + 2 * local_blocks, at + 4 * local_blocks))

        first, second = offsets[step, 0], offsets[step, 1]
        left, right = columns[step, 0], columns[step, 1]
        b2, b3 = block - first, block - second
        b4, b5 = column_block(left), column_block(right)
        far = 3 * local_blocks
        slots = [far + vert_total, step, near(first), near(second), far + left, far + right]
        live = [
            block > 0,
            None,
            b2 > 0,
            (b3 > 0) & (b3 != b2),
            (b4 > 0) & (b4 < block) & (b4 != b2) & (b4 != b3),
            (b5 > 0) & (b5 < block) & (b5 != b2) & (b5 != b3) & (b5 != b4),
        ]
        spots = [pl.ds(pl.multiple_of(slot * BLK, BLK), BLK) for slot in slots]
        queries, grads = stacked(q_ref, here), stacked(do_ref, here)
        keys = jnp.concatenate([pool_k[spot, :] for spot in spots], axis=0)
        values = jnp.concatenate([pool_v[spot, :] for spot in spots], axis=0)
        score = lax.dot_general(keys, queries, contract_last, preferred_element_type=jnp.float32)
        product = lax.dot_general(values, grads, contract_last, preferred_element_type=jnp.float32)
        return live, spots, queries, grads, keys, score, product

    def weigh(live, score, product):
        scores, tops, weights, probs, dscores = [], [], [], [], []
        for number in range(6):
            part = score[number * BLK : (number + 1) * BLK] * scale_two
            if number == 1:
                part = jnp.where(seen, part, -FAR)
            scores.append(part)
            top = jnp.max(part, axis=0, keepdims=True)
            tops.append(top if number == 1 else jnp.where(live[number], top, -FAR))
        top = functools.reduce(jnp.maximum, tops)
        total, delta = 0.0, 0.0
        for number in range(6):
            weight = jnp.exp2(scores[number] - (top if number == 1 else jnp.where(live[number], top, FAR)))
            total = total + jnp.sum(weight, axis=0, keepdims=True)
            delta = delta + jnp.sum(weight * product[number * BLK : (number + 1) * BLK], axis=0, keepdims=True)
            weights.append(weight)
        inverse = 1.0 / total
        delta = delta * inverse
        for number in range(6):
            prob = weights[number] * inverse
            dscores.append((prob * (product[number * BLK : (number + 1) * BLK] - delta)).astype(jnp.bfloat16))
            probs.append(prob.astype(jnp.bfloat16))
        return jnp.concatenate(probs, axis=0), jnp.concatenate(dscores, axis=0)

    def finish(sub, spots, queries, grads, keys, prob, dscore):
        value_terms = jnp.dot(prob, grads, preferred_element_type=jnp.float32)
        key_terms = jnp.dot(dscore, queries, preferred_element_type=jnp.float32)
        dq = lax.dot_general(dscore, keys, contract_first, preferred_element_type=jnp.float32)
        dq = (dq * scale).astype(jnp.bfloat16)
        for number, spot in enumerate(spots):
            acc_v[spot, :] += value_terms[number * BLK : (number + 1) * BLK]
            acc_k[spot, :] += key_terms[number * BLK : (number + 1) * BLK]
        for g in range(group):
            dq_out[sub * BLK : (sub + 1) * BLK, g * HD : (g + 1) * HD] = dq[g * BLK : (g + 1) * BLK]

    begun = begin(0)
    for sub in range(together):
        live, spots, queries, grads, keys, score, product = begun
        if sub + 1 < together:
            begun = begin(sub + 1)
        prob, dscore = weigh(live, score, product)
        finish(sub, spots, queries, grads, keys, prob, dscore)

    for k, dq_ref in enumerate(dq_refs):

        @pl.when(turn_number // (share // together) == k)
        def _():
            dq_ref[...] = dq_out[...]

    @pl.when(turn_number == local_blocks // together - 1)
    def _():
        for side, (acc, factor) in enumerate(((acc_k, scale), (acc_v, 1.0))):
            prev_ref[side] = (acc[rows : 2 * rows, :] * factor).astype(jnp.bfloat16)
            back_ref[side] = (acc[2 * rows : 3 * rows, :] * factor).astype(jnp.bfloat16)
            own_ref[side] = acc[:rows, :] * factor

            def far_block(number):
                start = pl.multiple_of((3 * local_blocks + number) * BLK, BLK)
                return (acc[pl.ds(start, BLK), :] * factor).astype(jnp.bfloat16)

            if last:
                for ref, parity in ((far_refs[0], seq_index % 2), (far_refs[1], 1 - seq_index % 2)):
                    for plane in range(vert_total // 2):
                        ref[plane, side] = far_block(2 * plane + parity)
                    ref[vert_total // 2, side] = far_block(vert_total)
            else:
                sink = far_block(vert_total)
                for number in range(vert_total):
                    far_refs[0][number, 0, side] = far_block(number)
                    far_refs[0][number, 1, side] = sink


def attention(
    head, kv_local, heads, place, vertical, columns, offsets, queries, grad_out, kv_own, kv_column, kv_other, first_even, first_odd,
    kv_back, kv_even, kv_odd
):
    seq_len = queries.shape[0]
    local_blocks = seq_len // BLK
    width = queries.shape[1] // kv_local
    group = width // HD
    vert_total = vertical.shape[0]
    total_rows = 3 * seq_len + (vert_total + 1) * BLK
    anywhere = pl.BlockSpec(memory_space=pl.ANY)
    share = local_blocks // heads
    together = min(4, share)
    turns = share // together
    by_block = pl.BlockSpec((together * BLK, width), lambda i, place, *_: ((i // turns ^ place[1]) * turns + i % turns, head))

    def whole(*shape):
        return pl.BlockSpec(shape, lambda i, *_: (0,) * len(shape))

    def share_spec(k):
        return pl.BlockSpec((together * BLK, width), lambda i, *_: (jnp.clip(i - k * turns, 0, turns - 1), 0))

    near_shape = (2, seq_len, HD)
    block_shape = (2, BLK, HD)
    last = head + 1 == kv_local
    far_shapes = [(vert_total // 2 + 1, *block_shape)] * 2 if last else [(vert_total, 2, *block_shape)]
    flops = 2 * 5 * seq_len * group * 6 * BLK * HD
    outs = pl.pallas_call(
        functools.partial(attention_kernel, (local_blocks, group, vert_total, heads, head, last)),
        grid_spec=pltpu.PrefetchScalarGridSpec(
            num_scalar_prefetch=4,
            grid=(local_blocks // together,),
            in_specs=[by_block, by_block] + [anywhere] * 8,
            out_specs=[share_spec(k) for k in range(heads)]
            + [whole(*near_shape)] * 3
            + [whole(*shape) for shape in far_shapes],
            scratch_shapes=[
                pltpu.VMEM((total_rows, HD), jnp.bfloat16),
                pltpu.VMEM((total_rows, HD), jnp.bfloat16),
                pltpu.VMEM((total_rows, HD), jnp.float32),
                pltpu.VMEM((total_rows, HD), jnp.float32),
                pltpu.VMEM((together * BLK, width), jnp.bfloat16),
                pltpu.SemaphoreType.DMA((2 * (4 + vert_total),)),
            ],
        ),
        out_shape=[jax.ShapeDtypeStruct((seq_len // heads, width), jnp.bfloat16)] * heads
        + [jax.ShapeDtypeStruct(near_shape, jnp.float32)]
        + [jax.ShapeDtypeStruct(near_shape, jnp.bfloat16)] * 2
        + [jax.ShapeDtypeStruct(shape, jnp.bfloat16) for shape in far_shapes],
        compiler_params=pltpu.CompilerParams(vmem_limit_bytes=50 * 1024 * 1024),
        cost_estimate=pl.CostEstimate(
            flops=4 * flops, bytes_accessed=20 * 1024 * 1024, transcendentals=seq_len * group * 6 * BLK
        ),
        name="attention",
    )(place, vertical, columns, offsets, queries, grad_out, kv_own, kv_column, kv_other, first_even, first_odd, kv_back, kv_even, kv_odd)
    return outs[:heads], *outs[heads:]


def queries_kernel(heads, kv_local, place, *refs):
    for k in range(heads):
        for head in range(kv_local):
            piece = refs[k * kv_local + head]
            width = piece.shape[1]
            column = (place[1] ^ k) * kv_local + head
            refs[-1][:, pl.ds(pl.multiple_of(column * width, width), width)] = piece[...]


def assemble_queries(place, heads, kv_local, pieces):
    rows, width = pieces[0, 0].shape
    tile = min(rows, 128)
    count = heads * kv_local
    return pl.pallas_call(
        functools.partial(queries_kernel, heads, kv_local),
        grid_spec=pltpu.PrefetchScalarGridSpec(
            num_scalar_prefetch=1,
            grid=(rows // tile,),
            in_specs=[pl.BlockSpec((tile, width), lambda i, *_: (i, 0))] * count,
            out_specs=pl.BlockSpec((tile, width * count), lambda i, *_: (i, 0)),
        ),
        out_shape=jax.ShapeDtypeStruct((rows, width * count), jnp.bfloat16),
        name="assemble_queries",
    )(place, *(pieces[k, head] for k in range(heads) for head in range(kv_local)))


def pairs_kernel(heads, kv_local, place, *refs):
    k_out, v_out = refs[-2:]
    for k in range(heads):
        for head in range(kv_local):
            column = (place[1] ^ k) * kv_local + head
            spot = pl.ds(pl.multiple_of(column * HD, HD), HD)
            both = refs[k * kv_local + head]
            k_out[:, spot] = both[0]
            v_out[:, spot] = both[1]


def assemble_pairs(place, heads, kv_local, pieces):
    arrays = [pieces[k, head] for k in range(heads) for head in range(kv_local)]
    rows = arrays[0].shape[1]
    tile = min(rows, 256)
    out_shape = jax.ShapeDtypeStruct((rows, HD * heads * kv_local), jnp.bfloat16)
    return pl.pallas_call(
        functools.partial(pairs_kernel, heads, kv_local),
        grid_spec=pltpu.PrefetchScalarGridSpec(
            num_scalar_prefetch=1,
            grid=(rows // tile,),
            in_specs=[pl.BlockSpec((2, tile, HD), lambda i, *_: (0, i, 0))] * len(arrays),
            out_specs=[pl.BlockSpec((tile, out_shape.shape[1]), lambda i, *_: (i, 0))] * 2,
        ),
        out_shape=[out_shape] * 2,
        name="assemble_pairs",
    )(place, *arrays)


def after(value, *others):
    return lax.optimization_barrier((value, others))[0]


def shards(queries, keys, values, grad_out, vertical, columns, offsets):
    seq_len = queries.shape[0]
    seq_size = lax.axis_size("seq")
    heads = lax.axis_size("head")
    kv_local = keys.shape[1] // HD
    local_blocks = seq_len // BLK
    seq_index = lax.axis_index("seq")
    head_index = lax.axis_index("head")
    place = jnp.stack([seq_index, head_index]).astype(jnp.int32)
    odd = seq_index % 2 == 1

    def along(array, pairs, name):
        with jax.named_scope(name):
            return lax.ppermute(array, "seq", pairs)

    def across(array, k, name):
        with jax.named_scope(name):
            return lax.ppermute(array, "head", [(i, i ^ k) for i in range(heads)]) if k else array

    def shift(by, only=None):
        return [(i, i + by) for i in range(seq_size) if 0 <= i + by < seq_size and only in (None, i % 2)]

    exchange = [(i, i ^ 1) for i in range(seq_size)]
    own_vertical = lax.dynamic_slice_in_dim(vertical, seq_index * VERT_DEV, VERT_DEV)[0]
    kvs = [
        jnp.stack([keys[:, head * HD : (head + 1) * HD], values[:, head * HD : (head + 1) * HD]])
        for head in range(kv_local)
    ]
    mine = jnp.stack([lax.dynamic_slice_in_dim(kv, own_vertical * BLK, BLK, axis=1) for kv in kvs])
    sink = jnp.stack([kv[:, :BLK] for kv in kvs])
    groups = [list(range(0, seq_size, 2)), list(range(1, seq_size, 2))]

    def column_of(block, name):
        with jax.named_scope(name):
            wide = jnp.broadcast_to(block, (seq_size // 2, *block.shape))
            return lax.all_to_all(wide, "seq", split_axis=0, concat_axis=0, axis_index_groups=groups)

    first = jnp.where(seq_index == 0, sink, 0.0).astype(sink.dtype)
    first = sum((along(sink, [(0, at)], f"in_first{at}") for at in range(2, seq_size, 2)), first)
    first_other = along(first, [(at, at + 1) for at in range(0, seq_size, 2)], "in_first_pair")

    fetched = []
    for head, kv in enumerate(kvs):
        block = mine[head]
        if head:
            kv, block = after((kv, block), fetched[-1][1], fetched[-1][4])
            back, even = along(kv, shift(2), f"in_back{head}"), along(kv, shift(1), f"in_prev{head}")
            odd_prev = even
        else:
            back, even = along(kv, shift(2), f"in_back{head}"), along(kv, shift(1, 0), f"in_even{head}")
            odd_prev = along(back, shift(-1, 1), f"in_odd{head}")
        kv_column = column_of(block, f"in_column{head}")
        if not head:
            kv_column = after(kv_column, back)
        kv_other = along(kv_column, exchange, f"in_column_pair{head}")
        fetched.append((kv, back, even, odd_prev, kv_column, kv_other))

    planes = seq_size // 2
    query_pieces, pair_pieces, results, fars = {}, {}, [], []

    def onward(back, side):
        return (back.astype(jnp.float32) + jnp.where(odd, side.astype(jnp.float32), 0.0)).astype(jnp.bfloat16)

    for head, (kv, back, even, odd_prev, kv_column, kv_other) in enumerate(fetched):
        last = head + 1 == kv_local
        dqs, own, prev, back, *table = attention(
            head, kv_local, heads, place, vertical, columns, offsets, queries, grad_out, kv, kv_column, kv_other, first, first_other,
            back, even, odd_prev
        )
        if not last:
            with jax.named_scope(f"out_far{head}"):
                fars.append(lax.all_to_all(table[0], "seq", split_axis=0, concat_axis=0))
            for k in range(heads):
                query_pieces[k, head] = across(dqs[k], k, f"out_query{head}_{k}")
            results.append((own, along(prev, exchange, f"out_pair{head}"), back))
            continue
        keep, give = table
        if head:
            before = [query_pieces[k, head - 1] for k in range(heads)]
            fars, results = after((fars, results), dqs[0])
            prev, give, dqs = after((prev, give, dqs), before, fars, results)
        got = along(give, exchange, f"out_far_pair{head}")
        for k in range(2, heads):
            query_pieces[k, head] = across(dqs[k], k, f"out_query{head}_{k}")
        sent = [onward(back_before, side_before) for _, side_before, back_before in results]
        side = along(prev, exchange, f"out_pair{head}")
        side = after(side, [query_pieces[k, head] for k in range(2, heads)])
        results = [
            (own_before, side_before, along(piece, shift(-2), f"out_onward{at}"))
            for at, ((own_before, side_before, _), piece) in enumerate(zip(results, sent))
        ]
        far_sum = (keep.astype(jnp.float32) + got.astype(jnp.float32)).astype(jnp.bfloat16)
        far_sum = jnp.stack([far_sum[:planes], jnp.broadcast_to(far_sum[planes], far_sum[:planes].shape)], axis=1)
        with jax.named_scope("out_far"):
            fars.append(lax.all_to_all(far_sum, "seq", split_axis=0, concat_axis=0, axis_index_groups=groups))
        fars = [jnp.sum(terms.astype(jnp.float32), axis=0) for terms in fars]
        if heads > 1:
            query_pieces[1, head] = across(after(dqs[1], far_sum), 1, f"out_query{head}_1")
        query_pieces[0, head] = dqs[0]
        results.append((own, side, along(onward(back, side), shift(-2), f"out_onward{head}")))

    block_ids = jnp.arange(local_blocks)[None, :, None, None]
    for head, (own, side, returned) in enumerate(results):
        if head and head + 1 == kv_local:
            query_out = assemble_queries(place, heads, kv_local, query_pieces)
            returned = after(returned, query_out, list(pair_pieces.values()))
        elif kv_local == 1:
            query_out = assemble_queries(place, heads, kv_local, query_pieces)

        def blocked(array):
            return array.reshape(2, local_blocks, BLK, HD).astype(jnp.float32)

        total = blocked(own) + (jnp.where(odd, 0.0, blocked(side)) + blocked(returned))
        total = total + jnp.where(block_ids == own_vertical, fars[head][0][:, None], 0.0)
        total = total + jnp.where((block_ids == 0) & (seq_index == 0), fars[head][1][:, None], 0.0)
        total = total.astype(jnp.bfloat16).reshape(2, heads, -1, HD)
        for k in range(heads):
            piece = lax.dynamic_index_in_dim(total, head_index ^ k, 1, keepdims=False)
            pair_pieces[k, head] = across(piece, k, f"out_pairs{head}_{k}")
    return (query_out, *assemble_pairs(place, heads, kv_local, pair_pieces))


def solution(mesh):
    return jax.shard_map(
        shards,
        mesh=mesh,
        in_specs=(
            P("seq", "head"),
            P("seq", "head"),
            P("seq", "head"),
            P("seq", "head"),
            P(),
            P("seq", None),
            P("seq", None),
        ),
        out_specs=(P(("seq", "head"), None), P(("seq", "head"), None), P(("seq", "head"), None)),
        check_vma=False,
    )
```

```python
import functools
import math

import jax
import jax.numpy as jnp
from jax import lax
from jax.experimental import pallas as pl
from jax.experimental.pallas import tpu as pltpu
from jax.sharding import PartitionSpec as P

HD = 128
BLK = 128
VERT_DEV = 1
FAR = 1e30


def attention_kernel(dims, place, vertical, columns, offsets, *refs):
    local_blocks, group, vert_total, heads, head, last = dims
    refs = list(refs)

    def take(count):
        taken = refs[:count]
        del refs[:count]
        return taken

    q_ref, do_ref, kv_own, kv_column, kv_other, first_even, first_odd = take(7)
    kv_back, kv_even, kv_odd = take(3)
    dq_refs, (own_ref, prev_ref, back_ref), far_refs = take(heads), take(3), take(2 if last else 1)
    pool_k, pool_v, acc_k, acc_v, dq_out, sems = refs
    turn_number = pl.program_id(0)
    seq_index, head_index = place[0], place[1]
    share = local_blocks // heads
    together = min(4, share)
    turns = share // together
    step_base = ((turn_number // turns ^ head_index) * turns + lax.rem(turn_number, turns)) * together
    rows = local_blocks * BLK
    scale = 1.0 / math.sqrt(HD)

    @pl.when(turn_number == 0)
    def _():
        def copies(prev, parity):
            parts = [(kv_own, 0), (prev, rows), (kv_back, 2 * rows)]
            made = []
            for side, pool in enumerate((pool_k, pool_v)):
                for ref, start in parts:
                    made.append((ref.at[side], pool.at[pl.ds(start, ref.shape[1])]))
                for ref, number in ((kv_column, parity), (kv_other, 1 - parity)):
                    for plane in range(vert_total // 2):
                        into = pool.at[pl.ds(3 * rows + (2 * plane + number) * BLK, BLK)]
                        made.append((ref.at[plane, side], into))
                source = first_odd if parity else first_even
                made.append((source.at[head, side], pool.at[pl.ds(3 * rows + vert_total * BLK, BLK)]))
            return [pltpu.make_async_copy(*ends, sems.at[at]) for at, ends in enumerate(made)]

        odd = lax.rem(seq_index, 2) == 1
        ways = ((odd, kv_even, 1), (jnp.logical_not(odd), kv_odd, 0))
        for way, prev, parity in ways:

            @pl.when(way)
            def _():
                for copy in copies(prev, parity):
                    copy.start()

        acc_k[...] = jnp.zeros_like(acc_k)
        acc_v[...] = jnp.zeros_like(acc_v)
        for way, prev, parity in ways:

            @pl.when(way)
            def _():
                for copy in copies(prev, parity):
                    copy.wait()

    scale_two = scale * math.log2(math.e)
    contract_last = (((1,), (1,)), ((), ()))
    contract_first = (((0,), (0,)), ((), ()))
    width = group * BLK
    seen = lax.broadcasted_iota(jnp.int32, (BLK, width), 0) <= lax.broadcasted_iota(jnp.int32, (BLK, width), 1) % BLK

    def column_block(column):
        return column // VERT_DEV * local_blocks + vertical[column]

    def stacked(ref, here):
        return jnp.concatenate([ref[here, g * HD : (g + 1) * HD] for g in range(group)], axis=0)

    def begin(sub):
        step = step_base + sub
        block = seq_index * local_blocks + step
        here = slice(sub * BLK, (sub + 1) * BLK)

        def near(offset):
            at = step - offset
            return jnp.where(at >= 0, at, jnp.where(at >= -local_blocks, at + 2 * local_blocks, at + 4 * local_blocks))

        first, second = offsets[step, 0], offsets[step, 1]
        left, right = columns[step, 0], columns[step, 1]
        b2, b3 = block - first, block - second
        b4, b5 = column_block(left), column_block(right)
        far = 3 * local_blocks
        slots = [far + vert_total, step, near(first), near(second), far + left, far + right]
        live = [
            block > 0,
            None,
            b2 > 0,
            (b3 > 0) & (b3 != b2),
            (b4 > 0) & (b4 < block) & (b4 != b2) & (b4 != b3),
            (b5 > 0) & (b5 < block) & (b5 != b2) & (b5 != b3) & (b5 != b4),
        ]
        spots = [pl.ds(pl.multiple_of(slot * BLK, BLK), BLK) for slot in slots]
        queries, grads = stacked(q_ref, here), stacked(do_ref, here)
        keys = jnp.concatenate([pool_k[spot, :] for spot in spots], axis=0)
        values = jnp.concatenate([pool_v[spot, :] for spot in spots], axis=0)
        score = lax.dot_general(keys, queries, contract_last, preferred_element_type=jnp.float32)
        product = lax.dot_general(values, grads, contract_last, preferred_element_type=jnp.float32)
        return live, spots, queries, grads, keys, score, product

    def weigh(live, score, product):
        scores, tops, weights, probs, dscores = [], [], [], [], []
        for number in range(6):
            part = score[number * BLK : (number + 1) * BLK] * scale_two
            if number == 1:
                part = jnp.where(seen, part, -FAR)
            scores.append(part)
            top = jnp.max(part, axis=0, keepdims=True)
            tops.append(top if number == 1 else jnp.where(live[number], top, -FAR))
        top = functools.reduce(jnp.maximum, tops)
        total, delta = 0.0, 0.0
        for number in range(6):
            weight = jnp.exp2(scores[number] - (top if number == 1 else jnp.where(live[number], top, FAR)))
            total = total + jnp.sum(weight, axis=0, keepdims=True)
            delta = delta + jnp.sum(weight * product[number * BLK : (number + 1) * BLK], axis=0, keepdims=True)
            weights.append(weight)
        inverse = 1.0 / total
        delta = delta * inverse
        for number in range(6):
            prob = (weights[number] * inverse).astype(jnp.bfloat16)
            dscores.append(prob * (product[number * BLK : (number + 1) * BLK] - delta).astype(jnp.bfloat16))
            probs.append(prob)
        return jnp.concatenate(probs, axis=0), jnp.concatenate(dscores, axis=0)

    def finish(sub, spots, queries, grads, keys, prob, dscore):
        value_terms = jnp.dot(prob, grads, preferred_element_type=jnp.float32)
        key_terms = jnp.dot(dscore, queries, preferred_element_type=jnp.float32)
        dq = lax.dot_general(dscore, keys, contract_first, preferred_element_type=jnp.float32)
        dq = (dq * scale).astype(jnp.bfloat16)
        for number, spot in enumerate(spots):
            acc_v[spot, :] += value_terms[number * BLK : (number + 1) * BLK]
            acc_k[spot, :] += key_terms[number * BLK : (number + 1) * BLK]
        for g in range(group):
            dq_out[sub * BLK : (sub + 1) * BLK, g * HD : (g + 1) * HD] = dq[g * BLK : (g + 1) * BLK]

    begun = begin(0)
    for sub in range(together):
        live, spots, queries, grads, keys, score, product = begun
        if sub + 1 < together:
            begun = begin(sub + 1)
        prob, dscore = weigh(live, score, product)
        finish(sub, spots, queries, grads, keys, prob, dscore)

    for k, dq_ref in enumerate(dq_refs):

        @pl.when(turn_number // (share // together) == k)
        def _():
            dq_ref[...] = dq_out[...]

    @pl.when(turn_number == local_blocks // together - 1)
    def _():
        for side, (acc, factor) in enumerate(((acc_k, scale), (acc_v, 1.0))):
            prev_ref[side] = (acc[rows : 2 * rows, :] * factor).astype(jnp.bfloat16)
            back_ref[side] = (acc[2 * rows : 3 * rows, :] * factor).astype(jnp.bfloat16)
            own_ref[side] = (acc[:rows, :] * factor).astype(jnp.bfloat16)

            def far_block(number):
                start = pl.multiple_of((3 * local_blocks + number) * BLK, BLK)
                return (acc[pl.ds(start, BLK), :] * factor).astype(jnp.bfloat16)

            if last:
                for ref, parity in ((far_refs[0], seq_index % 2), (far_refs[1], 1 - seq_index % 2)):
                    for plane in range(vert_total // 2):
                        ref[plane, side] = far_block(2 * plane + parity)
                    ref[vert_total // 2, side] = far_block(vert_total)
            else:
                sink = far_block(vert_total)
                for number in range(vert_total):
                    far_refs[0][number, 0, side] = far_block(number)
                    far_refs[0][number, 1, side] = sink


def attention(
    head, kv_local, heads, place, vertical, columns, offsets, queries, grad_out, kv_own, kv_column, kv_other, first_even, first_odd,
    kv_back, kv_even, kv_odd
):
    seq_len = queries.shape[0]
    local_blocks = seq_len // BLK
    width = queries.shape[1] // kv_local
    group = width // HD
    vert_total = vertical.shape[0]
    total_rows = 3 * seq_len + (vert_total + 1) * BLK
    anywhere = pl.BlockSpec(memory_space=pl.ANY)
    share = local_blocks // heads
    together = min(4, share)
    turns = share // together
    by_block = pl.BlockSpec((together * BLK, width), lambda i, place, *_: ((i // turns ^ place[1]) * turns + i % turns, head))

    def whole(*shape):
        return pl.BlockSpec(shape, lambda i, *_: (0,) * len(shape))

    def share_spec(k):
        return pl.BlockSpec((together * BLK, width), lambda i, *_: (jnp.clip(i - k * turns, 0, turns - 1), 0))

    near_shape = (2, seq_len, HD)
    block_shape = (2, BLK, HD)
    last = head + 1 == kv_local
    far_shapes = [(vert_total // 2 + 1, *block_shape)] * 2 if last else [(vert_total, 2, *block_shape)]
    flops = 2 * 5 * seq_len * group * 6 * BLK * HD
    outs = pl.pallas_call(
        functools.partial(attention_kernel, (local_blocks, group, vert_total, heads, head, last)),
        grid_spec=pltpu.PrefetchScalarGridSpec(
            num_scalar_prefetch=4,
            grid=(local_blocks // together,),
            in_specs=[by_block, by_block] + [anywhere] * 8,
            out_specs=[share_spec(k) for k in range(heads)]
            + [whole(*near_shape)] * 3
            + [whole(*shape) for shape in far_shapes],
            scratch_shapes=[
                pltpu.VMEM((total_rows, HD), jnp.bfloat16),
                pltpu.VMEM((total_rows, HD), jnp.bfloat16),
                pltpu.VMEM((total_rows, HD), jnp.float32),
                pltpu.VMEM((total_rows, HD), jnp.float32),
                pltpu.VMEM((together * BLK, width), jnp.bfloat16),
                pltpu.SemaphoreType.DMA((2 * (4 + vert_total),)),
            ],
        ),
        out_shape=[jax.ShapeDtypeStruct((seq_len // heads, width), jnp.bfloat16)] * heads
        + [jax.ShapeDtypeStruct(near_shape, jnp.bfloat16)] * 3
        + [jax.ShapeDtypeStruct(shape, jnp.bfloat16) for shape in far_shapes],
        compiler_params=pltpu.CompilerParams(vmem_limit_bytes=50 * 1024 * 1024),
        cost_estimate=pl.CostEstimate(
            flops=4 * flops, bytes_accessed=20 * 1024 * 1024, transcendentals=seq_len * group * 6 * BLK
        ),
        name="attention",
    )(place, vertical, columns, offsets, queries, grad_out, kv_own, kv_column, kv_other, first_even, first_odd, kv_back, kv_even, kv_odd)
    return outs[:heads], *outs[heads:]


def queries_kernel(heads, kv_local, place, *refs):
    for k in range(heads):
        for head in range(kv_local):
            piece = refs[k * kv_local + head]
            width = piece.shape[1]
            column = (place[1] ^ k) * kv_local + head
            refs[-1][:, pl.ds(pl.multiple_of(column * width, width), width)] = piece[...]


def assemble_queries(place, heads, kv_local, pieces):
    rows, width = pieces[0, 0].shape
    tile = min(rows, 128)
    count = heads * kv_local
    return pl.pallas_call(
        functools.partial(queries_kernel, heads, kv_local),
        grid_spec=pltpu.PrefetchScalarGridSpec(
            num_scalar_prefetch=1,
            grid=(rows // tile,),
            in_specs=[pl.BlockSpec((tile, width), lambda i, *_: (i, 0))] * count,
            out_specs=pl.BlockSpec((tile, width * count), lambda i, *_: (i, 0)),
        ),
        out_shape=jax.ShapeDtypeStruct((rows, width * count), jnp.bfloat16),
        name="assemble_queries",
    )(place, *(pieces[k, head] for k in range(heads) for head in range(kv_local)))


def pairs_kernel(heads, kv_local, place, *refs):
    k_out, v_out = refs[-2:]
    for k in range(heads):
        for head in range(kv_local):
            column = (place[1] ^ k) * kv_local + head
            spot = pl.ds(pl.multiple_of(column * HD, HD), HD)
            both = refs[k * kv_local + head]
            k_out[:, spot] = both[0]
            v_out[:, spot] = both[1]


def assemble_pairs(place, heads, kv_local, pieces):
    arrays = [pieces[k, head] for k in range(heads) for head in range(kv_local)]
    rows = arrays[0].shape[1]
    tile = min(rows, 256)
    out_shape = jax.ShapeDtypeStruct((rows, HD * heads * kv_local), jnp.bfloat16)
    return pl.pallas_call(
        functools.partial(pairs_kernel, heads, kv_local),
        grid_spec=pltpu.PrefetchScalarGridSpec(
            num_scalar_prefetch=1,
            grid=(rows // tile,),
            in_specs=[pl.BlockSpec((2, tile, HD), lambda i, *_: (0, i, 0))] * len(arrays),
            out_specs=[pl.BlockSpec((tile, out_shape.shape[1]), lambda i, *_: (i, 0))] * 2,
        ),
        out_shape=[out_shape] * 2,
        name="assemble_pairs",
    )(place, *arrays)


def after(value, *others):
    return lax.optimization_barrier((value, others))[0]


def shards(queries, keys, values, grad_out, vertical, columns, offsets):
    seq_len = queries.shape[0]
    seq_size = lax.axis_size("seq")
    heads = lax.axis_size("head")
    kv_local = keys.shape[1] // HD
    local_blocks = seq_len // BLK
    seq_index = lax.axis_index("seq")
    head_index = lax.axis_index("head")
    place = jnp.stack([seq_index, head_index]).astype(jnp.int32)
    odd = seq_index % 2 == 1

    def along(array, pairs, name):
        with jax.named_scope(name):
            return lax.ppermute(array, "seq", pairs)

    def across(array, k, name):
        with jax.named_scope(name):
            return lax.ppermute(array, "head", [(i, i ^ k) for i in range(heads)]) if k else array

    def shift(by, only=None):
        return [(i, i + by) for i in range(seq_size) if 0 <= i + by < seq_size and only in (None, i % 2)]

    exchange = [(i, i ^ 1) for i in range(seq_size)]
    own_vertical = lax.dynamic_slice_in_dim(vertical, seq_index * VERT_DEV, VERT_DEV)[0]
    kvs = [
        jnp.stack([keys[:, head * HD : (head + 1) * HD], values[:, head * HD : (head + 1) * HD]])
        for head in range(kv_local)
    ]
    mine = jnp.stack([lax.dynamic_slice_in_dim(kv, own_vertical * BLK, BLK, axis=1) for kv in kvs])
    sink = jnp.stack([kv[:, :BLK] for kv in kvs])
    groups = [list(range(0, seq_size, 2)), list(range(1, seq_size, 2))]

    def column_of(block, name):
        with jax.named_scope(name):
            wide = jnp.broadcast_to(block, (seq_size // 2, *block.shape))
            return lax.all_to_all(wide, "seq", split_axis=0, concat_axis=0, axis_index_groups=groups)

    first = jnp.where(seq_index == 0, sink, 0.0).astype(sink.dtype)
    first = sum((along(sink, [(0, at)], f"in_first{at}") for at in range(2, seq_size, 2)), first)
    first_other = along(first, [(at, at + 1) for at in range(0, seq_size, 2)], "in_first_pair")

    fetched = []
    for head, kv in enumerate(kvs):
        block = mine[head]
        if head:
            kv, block = after((kv, block), fetched[-1][1], fetched[-1][4])
            back, even = along(kv, shift(2), f"in_back{head}"), along(kv, shift(1), f"in_prev{head}")
            odd_prev = even
        else:
            back, even = along(kv, shift(2), f"in_back{head}"), along(kv, shift(1, 0), f"in_even{head}")
            odd_prev = along(back, shift(-1, 1), f"in_odd{head}")
        kv_column = column_of(block, f"in_column{head}")
        if not head:
            kv_column = after(kv_column, back)
        kv_other = along(kv_column, exchange, f"in_column_pair{head}")
        fetched.append((kv, back, even, odd_prev, kv_column, kv_other))

    planes = seq_size // 2
    query_pieces, pair_pieces, results, fars = {}, {}, [], []

    def onward(back, side):
        return (back.astype(jnp.float32) + jnp.where(odd, side.astype(jnp.float32), 0.0)).astype(jnp.bfloat16)

    for head, (kv, back, even, odd_prev, kv_column, kv_other) in enumerate(fetched):
        last = head + 1 == kv_local
        dqs, own, prev, back, *table = attention(
            head, kv_local, heads, place, vertical, columns, offsets, queries, grad_out, kv, kv_column, kv_other, first, first_other,
            back, even, odd_prev
        )
        if not last:
            with jax.named_scope(f"out_far{head}"):
                fars.append(lax.all_to_all(table[0], "seq", split_axis=0, concat_axis=0))
            for k in range(heads):
                query_pieces[k, head] = across(dqs[k], k, f"out_query{head}_{k}")
            results.append((own, along(prev, exchange, f"out_pair{head}"), back))
            continue
        keep, give = table
        if head:
            before = [query_pieces[k, head - 1] for k in range(heads)]
            fars, results = after((fars, results), dqs[0])
            prev, give, dqs = after((prev, give, dqs), before, fars, results)
        got = along(give, exchange, f"out_far_pair{head}")
        for k in range(2, heads):
            query_pieces[k, head] = across(dqs[k], k, f"out_query{head}_{k}")
        sent = [onward(back_before, side_before) for _, side_before, back_before in results]
        side = along(prev, exchange, f"out_pair{head}")
        side = after(side, [query_pieces[k, head] for k in range(2, heads)])
        results = [
            (own_before, side_before, along(piece, shift(-2), f"out_onward{at}"))
            for at, ((own_before, side_before, _), piece) in enumerate(zip(results, sent))
        ]
        far_sum = (keep.astype(jnp.float32) + got.astype(jnp.float32)).astype(jnp.bfloat16)
        far_sum = jnp.stack([far_sum[:planes], jnp.broadcast_to(far_sum[planes], far_sum[:planes].shape)], axis=1)
        with jax.named_scope("out_far"):
            fars.append(lax.all_to_all(far_sum, "seq", split_axis=0, concat_axis=0, axis_index_groups=groups))
        fars = [jnp.sum(terms.astype(jnp.float32), axis=0) for terms in fars]
        if heads > 1:
            query_pieces[1, head] = across(after(dqs[1], far_sum), 1, f"out_query{head}_1")
        query_pieces[0, head] = dqs[0]
        results.append((own, side, along(onward(back, side), shift(-2), f"out_onward{head}")))

    block_ids = jnp.arange(local_blocks)[None, :, None, None]
    for head, (own, side, returned) in enumerate(results):
        if head and head + 1 == kv_local:
            query_out = assemble_queries(place, heads, kv_local, query_pieces)
            returned = after(returned, query_out, list(pair_pieces.values()))
        elif kv_local == 1:
            query_out = assemble_queries(place, heads, kv_local, query_pieces)

        def blocked(array):
            return array.reshape(2, local_blocks, BLK, HD).astype(jnp.float32)

        total = blocked(own) + (jnp.where(odd, 0.0, blocked(side)) + blocked(returned))
        total = total + jnp.where(block_ids == own_vertical, fars[head][0][:, None], 0.0)
        total = total + jnp.where((block_ids == 0) & (seq_index == 0), fars[head][1][:, None], 0.0)
        total = total.astype(jnp.bfloat16).reshape(2, heads, -1, HD)
        for k in range(heads):
            piece = lax.dynamic_index_in_dim(total, head_index ^ k, 1, keepdims=False)
            pair_pieces[k, head] = across(piece, k, f"out_pairs{head}_{k}")
    return (query_out, *assemble_pairs(place, heads, kv_local, pair_pieces))


def solution(mesh):
    return jax.shard_map(
        shards,
        mesh=mesh,
        in_specs=(
            P("seq", "head"),
            P("seq", "head"),
            P("seq", "head"),
            P("seq", "head"),
            P(),
            P("seq", None),
            P("seq", None),
        ),
        out_specs=(P(("seq", "head"), None), P(("seq", "head"), None), P(("seq", "head"), None)),
        check_vma=False,
    )
```

```python
import functools
import math

import jax
import jax.numpy as jnp
from jax import lax
from jax.experimental import pallas as pl
from jax.experimental.pallas import tpu as pltpu
from jax.sharding import PartitionSpec as P

HD = 128
BLK = 128
VERT_DEV = 1
FAR = 1e30


def attention_kernel(dims, place, vertical, columns, offsets, *refs):
    local_blocks, group, vert_total, heads, head, last = dims
    refs = list(refs)

    def take(count):
        taken = refs[:count]
        del refs[:count]
        return taken

    q_ref, do_ref, kv_own, kv_column, kv_other, first_even, first_odd = take(7)
    kv_back, kv_even, kv_odd = take(3)
    dq_refs, (own_ref, prev_ref, back_ref), far_refs = take(heads), take(3), take(2 if last else 1)
    pool_k, pool_v, acc_k, acc_v, dq_out, sems = refs
    turn_number = pl.program_id(0)
    seq_index, head_index = place[0], place[1]
    share = local_blocks // heads
    together = min(4, share)
    turns = share // together
    step_base = ((turn_number // turns ^ head_index) * turns + lax.rem(turn_number, turns)) * together
    rows = local_blocks * BLK
    scale = 1.0 / math.sqrt(HD)

    @pl.when(turn_number == 0)
    def _():
        def copies(prev, parity):
            parts = [(kv_own, 0), (prev, rows), (kv_back, 2 * rows)]
            made = []
            for side, pool in enumerate((pool_k, pool_v)):
                for ref, start in parts:
                    made.append((ref.at[side], pool.at[pl.ds(start, ref.shape[1])]))
                for ref, number in ((kv_column, parity), (kv_other, 1 - parity)):
                    for plane in range(vert_total // 2):
                        into = pool.at[pl.ds(3 * rows + (2 * plane + number) * BLK, BLK)]
                        made.append((ref.at[plane, side], into))
                source = first_odd if parity else first_even
                made.append((source.at[head, side], pool.at[pl.ds(3 * rows + vert_total * BLK, BLK)]))
            return [pltpu.make_async_copy(*ends, sems.at[at]) for at, ends in enumerate(made)]

        odd = lax.rem(seq_index, 2) == 1
        ways = ((odd, kv_even, 1), (jnp.logical_not(odd), kv_odd, 0))
        for way, prev, parity in ways:

            @pl.when(way)
            def _():
                for copy in copies(prev, parity):
                    copy.start()

        acc_k[...] = jnp.zeros_like(acc_k)
        acc_v[...] = jnp.zeros_like(acc_v)
        for way, prev, parity in ways:

            @pl.when(way)
            def _():
                for copy in copies(prev, parity):
                    copy.wait()

    scale_two = scale * math.log2(math.e)
    contract_last = (((1,), (1,)), ((), ()))
    contract_first = (((0,), (0,)), ((), ()))
    width = group * BLK
    seen = lax.broadcasted_iota(jnp.int32, (BLK, width), 0) <= lax.broadcasted_iota(jnp.int32, (BLK, width), 1) % BLK

    def column_block(column):
        return column // VERT_DEV * local_blocks + vertical[column]

    def stacked(ref, here):
        return jnp.concatenate([ref[here, g * HD : (g + 1) * HD] for g in range(group)], axis=0)

    def begin(sub):
        step = step_base + sub
        block = seq_index * local_blocks + step
        here = slice(sub * BLK, (sub + 1) * BLK)

        def near(offset):
            at = step - offset
            return jnp.where(at >= 0, at, jnp.where(at >= -local_blocks, at + 2 * local_blocks, at + 4 * local_blocks))

        first, second = offsets[step, 0], offsets[step, 1]
        left, right = columns[step, 0], columns[step, 1]
        b2, b3 = block - first, block - second
        b4, b5 = column_block(left), column_block(right)
        far = 3 * local_blocks
        slots = [far + vert_total, step, near(first), near(second), far + left, far + right]
        live = [
            block > 0,
            None,
            b2 > 0,
            (b3 > 0) & (b3 != b2),
            (b4 > 0) & (b4 < block) & (b4 != b2) & (b4 != b3),
            (b5 > 0) & (b5 < block) & (b5 != b2) & (b5 != b3) & (b5 != b4),
        ]
        spots = [pl.ds(pl.multiple_of(slot * BLK, BLK), BLK) for slot in slots]
        queries, grads = stacked(q_ref, here), stacked(do_ref, here)
        keys = jnp.concatenate([pool_k[spot, :] for spot in spots], axis=0)
        values = jnp.concatenate([pool_v[spot, :] for spot in spots], axis=0)
        score = lax.dot_general(keys, queries, contract_last, preferred_element_type=jnp.float32)
        product = lax.dot_general(values, grads, contract_last, preferred_element_type=jnp.float32)
        return live, spots, queries, grads, keys, score, product

    def weigh(live, score, product):
        scores, tops, weights, probs, dscores = [], [], [], [], []
        for number in range(6):
            part = score[number * BLK : (number + 1) * BLK] * scale_two
            if number == 1:
                part = jnp.where(seen, part, -FAR)
            scores.append(part)
            top = jnp.max(part, axis=0, keepdims=True)
            tops.append(top if number == 1 else jnp.where(live[number], top, -FAR))
        top = functools.reduce(jnp.maximum, tops)
        total, delta = 0.0, 0.0
        for number in range(6):
            weight = jnp.exp2(scores[number] - (top if number == 1 else jnp.where(live[number], top, FAR)))
            total = total + jnp.sum(weight, axis=0, keepdims=True)
            delta = delta + jnp.sum(weight * product[number * BLK : (number + 1) * BLK], axis=0, keepdims=True)
            weights.append(weight)
        inverse = 1.0 / total
        delta = delta * inverse
        for number in range(6):
            prob = (weights[number] * inverse).astype(jnp.bfloat16)
            dscores.append(prob * (product[number * BLK : (number + 1) * BLK] - delta).astype(jnp.bfloat16))
            probs.append(prob)
        return jnp.concatenate(probs, axis=0), jnp.concatenate(dscores, axis=0)

    def finish(sub, spots, queries, grads, keys, prob, dscore):
        value_terms = jnp.dot(prob, grads, preferred_element_type=jnp.float32)
        key_terms = jnp.dot(dscore, queries, preferred_element_type=jnp.float32)
        dq = lax.dot_general(dscore, keys, contract_first, preferred_element_type=jnp.float32)
        dq = (dq * scale).astype(jnp.bfloat16)
        for number, spot in enumerate(spots):
            acc_v[spot, :] += value_terms[number * BLK : (number + 1) * BLK]
            acc_k[spot, :] += key_terms[number * BLK : (number + 1) * BLK]
        for g in range(group):
            dq_out[sub * BLK : (sub + 1) * BLK, g * HD : (g + 1) * HD] = dq[g * BLK : (g + 1) * BLK]

    begun = begin(0)
    for sub in range(together):
        live, spots, queries, grads, keys, score, product = begun
        if sub + 1 < together:
            begun = begin(sub + 1)
        prob, dscore = weigh(live, score, product)
        finish(sub, spots, queries, grads, keys, prob, dscore)

    for k, dq_ref in enumerate(dq_refs):

        @pl.when(turn_number // (share // together) == k)
        def _():
            dq_ref[...] = dq_out[...]

    @pl.when(turn_number == local_blocks // together - 1)
    def _():
        for side, (acc, factor) in enumerate(((acc_k, scale), (acc_v, 1.0))):
            prev_ref[side] = (acc[rows : 2 * rows, :] * factor).astype(jnp.bfloat16)
            back_ref[side] = (acc[2 * rows : 3 * rows, :] * factor).astype(jnp.bfloat16)
            own_ref[side] = (acc[:rows, :] * factor).astype(jnp.bfloat16)

            def far_block(number):
                start = pl.multiple_of((3 * local_blocks + number) * BLK, BLK)
                return (acc[pl.ds(start, BLK), :] * factor).astype(jnp.bfloat16)

            if last:
                for ref, parity in ((far_refs[0], seq_index % 2), (far_refs[1], 1 - seq_index % 2)):
                    for plane in range(vert_total // 2):
                        ref[plane, side] = far_block(2 * plane + parity)
                    ref[vert_total // 2, side] = far_block(vert_total)
            else:
                sink = far_block(vert_total)
                for number in range(vert_total):
                    far_refs[0][number, 0, side] = far_block(number)
                    far_refs[0][number, 1, side] = sink


def attention(
    head, kv_local, heads, place, vertical, columns, offsets, queries, grad_out, kv_own, kv_column, kv_other, first_even, first_odd,
    kv_back, kv_even, kv_odd
):
    seq_len = queries.shape[0]
    local_blocks = seq_len // BLK
    width = queries.shape[1] // kv_local
    group = width // HD
    vert_total = vertical.shape[0]
    total_rows = 3 * seq_len + (vert_total + 1) * BLK
    anywhere = pl.BlockSpec(memory_space=pl.ANY)
    share = local_blocks // heads
    together = min(4, share)
    turns = share // together
    by_block = pl.BlockSpec((together * BLK, width), lambda i, place, *_: ((i // turns ^ place[1]) * turns + i % turns, head))

    def whole(*shape):
        return pl.BlockSpec(shape, lambda i, *_: (0,) * len(shape))

    def share_spec(k):
        return pl.BlockSpec((together * BLK, width), lambda i, *_: (jnp.clip(i - k * turns, 0, turns - 1), 0))

    near_shape = (2, seq_len, HD)
    block_shape = (2, BLK, HD)
    last = head + 1 == kv_local
    far_shapes = [(vert_total // 2 + 1, *block_shape)] * 2 if last else [(vert_total, 2, *block_shape)]
    flops = 2 * 5 * seq_len * group * 6 * BLK * HD
    outs = pl.pallas_call(
        functools.partial(attention_kernel, (local_blocks, group, vert_total, heads, head, last)),
        grid_spec=pltpu.PrefetchScalarGridSpec(
            num_scalar_prefetch=4,
            grid=(local_blocks // together,),
            in_specs=[by_block, by_block] + [anywhere] * 8,
            out_specs=[share_spec(k) for k in range(heads)]
            + [whole(*near_shape)] * 3
            + [whole(*shape) for shape in far_shapes],
            scratch_shapes=[
                pltpu.VMEM((total_rows, HD), jnp.bfloat16),
                pltpu.VMEM((total_rows, HD), jnp.bfloat16),
                pltpu.VMEM((total_rows, HD), jnp.float32),
                pltpu.VMEM((total_rows, HD), jnp.float32),
                pltpu.VMEM((together * BLK, width), jnp.bfloat16),
                pltpu.SemaphoreType.DMA((2 * (4 + vert_total),)),
            ],
        ),
        out_shape=[jax.ShapeDtypeStruct((seq_len // heads, width), jnp.bfloat16)] * heads
        + [jax.ShapeDtypeStruct(near_shape, jnp.bfloat16)] * 3
        + [jax.ShapeDtypeStruct(shape, jnp.bfloat16) for shape in far_shapes],
        compiler_params=pltpu.CompilerParams(vmem_limit_bytes=50 * 1024 * 1024),
        cost_estimate=pl.CostEstimate(
            flops=4 * flops, bytes_accessed=20 * 1024 * 1024, transcendentals=seq_len * group * 6 * BLK
        ),
        name="attention",
    )(place, vertical, columns, offsets, queries, grad_out, kv_own, kv_column, kv_other, first_even, first_odd, kv_back, kv_even, kv_odd)
    return outs[:heads], *outs[heads:]


def queries_kernel(heads, kv_local, place, *refs):
    for k in range(heads):
        for head in range(kv_local):
            piece = refs[k * kv_local + head]
            width = piece.shape[1]
            column = (place[1] ^ k) * kv_local + head
            refs[-1][:, pl.ds(pl.multiple_of(column * width, width), width)] = piece[...]


def assemble_queries(place, heads, kv_local, pieces):
    rows, width = pieces[0, 0].shape
    tile = min(rows, 128)
    count = heads * kv_local
    return pl.pallas_call(
        functools.partial(queries_kernel, heads, kv_local),
        grid_spec=pltpu.PrefetchScalarGridSpec(
            num_scalar_prefetch=1,
            grid=(rows // tile,),
            in_specs=[pl.BlockSpec((tile, width), lambda i, *_: (i, 0))] * count,
            out_specs=pl.BlockSpec((tile, width * count), lambda i, *_: (i, 0)),
        ),
        out_shape=jax.ShapeDtypeStruct((rows, width * count), jnp.bfloat16),
        name="assemble_queries",
    )(place, *(pieces[k, head] for k in range(heads) for head in range(kv_local)))


def pairs_kernel(heads, kv_local, place, *refs):
    k_out, v_out = refs[-2:]
    for k in range(heads):
        for head in range(kv_local):
            column = (place[1] ^ k) * kv_local + head
            spot = pl.ds(pl.multiple_of(column * HD, HD), HD)
            both = refs[k * kv_local + head]
            k_out[:, spot] = both[0]
            v_out[:, spot] = both[1]


def assemble_pairs(place, heads, kv_local, pieces):
    arrays = [pieces[k, head] for k in range(heads) for head in range(kv_local)]
    rows = arrays[0].shape[1]
    tile = min(rows, 256)
    out_shape = jax.ShapeDtypeStruct((rows, HD * heads * kv_local), jnp.bfloat16)
    return pl.pallas_call(
        functools.partial(pairs_kernel, heads, kv_local),
        grid_spec=pltpu.PrefetchScalarGridSpec(
            num_scalar_prefetch=1,
            grid=(rows // tile,),
            in_specs=[pl.BlockSpec((2, tile, HD), lambda i, *_: (0, i, 0))] * len(arrays),
            out_specs=[pl.BlockSpec((tile, out_shape.shape[1]), lambda i, *_: (i, 0))] * 2,
        ),
        out_shape=[out_shape] * 2,
        name="assemble_pairs",
    )(place, *arrays)


def after(value, *others):
    return lax.optimization_barrier((value, others))[0]


def shards(queries, keys, values, grad_out, vertical, columns, offsets):
    seq_len = queries.shape[0]
    seq_size = lax.axis_size("seq")
    heads = lax.axis_size("head")
    kv_local = keys.shape[1] // HD
    local_blocks = seq_len // BLK
    seq_index = lax.axis_index("seq")
    head_index = lax.axis_index("head")
    place = jnp.stack([seq_index, head_index]).astype(jnp.int32)
    odd = seq_index % 2 == 1

    def along(array, pairs, name):
        with jax.named_scope(name):
            return lax.ppermute(array, "seq", pairs)

    def across(array, k, name):
        with jax.named_scope(name):
            return lax.ppermute(array, "head", [(i, i ^ k) for i in range(heads)]) if k else array

    def shift(by, only=None):
        return [(i, i + by) for i in range(seq_size) if 0 <= i + by < seq_size and only in (None, i % 2)]

    exchange = [(i, i ^ 1) for i in range(seq_size)]
    own_vertical = lax.dynamic_slice_in_dim(vertical, seq_index * VERT_DEV, VERT_DEV)[0]
    kvs = [
        jnp.stack([keys[:, head * HD : (head + 1) * HD], values[:, head * HD : (head + 1) * HD]])
        for head in range(kv_local)
    ]
    mine = jnp.stack([lax.dynamic_slice_in_dim(kv, own_vertical * BLK, BLK, axis=1) for kv in kvs])
    sink = jnp.stack([kv[:, :BLK] for kv in kvs])
    groups = [list(range(0, seq_size, 2)), list(range(1, seq_size, 2))]

    def column_of(block, name):
        with jax.named_scope(name):
            wide = jnp.broadcast_to(block, (seq_size // 2, *block.shape))
            return lax.all_to_all(wide, "seq", split_axis=0, concat_axis=0, axis_index_groups=groups)

    first = jnp.where(seq_index == 0, sink, 0.0).astype(sink.dtype)
    first = sum((along(sink, [(0, at)], f"in_first{at}") for at in range(2, seq_size, 2)), first)
    first_other = along(first, [(at, at + 1) for at in range(0, seq_size, 2)], "in_first_pair")

    fetched = []
    for head, kv in enumerate(kvs):
        block = mine[head]
        if head:
            kv, block = after((kv, block), fetched[-1][1], fetched[-1][4])
            back, even = along(kv, shift(2), f"in_back{head}"), along(kv, shift(1), f"in_prev{head}")
            odd_prev = even
        else:
            back, even = along(kv, shift(2), f"in_back{head}"), along(kv, shift(1, 0), f"in_even{head}")
            odd_prev = along(back, shift(-1, 1), f"in_odd{head}")
        kv_column = column_of(block, f"in_column{head}")
        if not head:
            kv_column = after(kv_column, back)
        kv_other = along(kv_column, exchange, f"in_column_pair{head}")
        fetched.append((kv, back, even, odd_prev, kv_column, kv_other))

    planes = seq_size // 2
    query_pieces, pair_pieces, results, fars = {}, {}, [], []

    def onward(back, side):
        return (back.astype(jnp.float32) + jnp.where(odd, side.astype(jnp.float32), 0.0)).astype(jnp.bfloat16)

    for head, (kv, back, even, odd_prev, kv_column, kv_other) in enumerate(fetched):
        last = head + 1 == kv_local
        dqs, own, prev, back, *table = attention(
            head, kv_local, heads, place, vertical, columns, offsets, queries, grad_out, kv, kv_column, kv_other, first, first_other,
            back, even, odd_prev
        )
        if not last:
            with jax.named_scope(f"out_far{head}"):
                fars.append(lax.all_to_all(table[0], "seq", split_axis=0, concat_axis=0))
            for k in range(heads):
                query_pieces[k, head] = across(dqs[k], k, f"out_query{head}_{k}")
            results.append((own, along(prev, exchange, f"out_pair{head}"), back))
            continue
        keep, give = table
        if head:
            before = [query_pieces[k, head - 1] for k in range(heads)]
            fars, results = after((fars, results), dqs[0])
            prev, give, dqs = after((prev, give, dqs), before, fars, results)
        got = along(give, exchange, f"out_far_pair{head}")
        for k in range(2, heads):
            query_pieces[k, head] = across(dqs[k], k, f"out_query{head}_{k}")
        sent = [onward(back_before, side_before) for _, side_before, back_before in results]
        side = along(prev, exchange, f"out_pair{head}")
        side = after(side, [query_pieces[k, head] for k in range(2, heads)])
        results = [
            (own_before, side_before, along(piece, shift(-2), f"out_onward{at}"))
            for at, ((own_before, side_before, _), piece) in enumerate(zip(results, sent))
        ]
        far_sum = (keep.astype(jnp.float32) + got.astype(jnp.float32)).astype(jnp.bfloat16)
        with jax.named_scope("out_far"):
            far = lax.all_to_all(far_sum[:planes], "seq", split_axis=0, concat_axis=0, axis_index_groups=groups)
        first = far_sum[planes].astype(jnp.float32)
        for at in range(2, seq_size, 2):
            first = first + along(far_sum[planes], [(at, 0)], f"out_first{at}").astype(jnp.float32)
        fars = [jnp.sum(terms.astype(jnp.float32), axis=0) for terms in fars]
        fars.append((jnp.sum(far.astype(jnp.float32), axis=0), first))
        if heads > 1:
            query_pieces[1, head] = across(after(dqs[1], far_sum), 1, f"out_query{head}_1")
        query_pieces[0, head] = dqs[0]
        results.append((own, side, along(onward(back, side), shift(-2), f"out_onward{head}")))

    block_ids = jnp.arange(local_blocks)[None, :, None, None]
    for head, (own, side, returned) in enumerate(results):
        if head and head + 1 == kv_local:
            query_out = assemble_queries(place, heads, kv_local, query_pieces)
            returned = after(returned, query_out, list(pair_pieces.values()))
        elif kv_local == 1:
            query_out = assemble_queries(place, heads, kv_local, query_pieces)

        def blocked(array):
            return array.reshape(2, local_blocks, BLK, HD).astype(jnp.float32)

        total = blocked(own) + (jnp.where(odd, 0.0, blocked(side)) + blocked(returned))
        total = total + jnp.where(block_ids == own_vertical, fars[head][0][:, None], 0.0)
        total = total + jnp.where((block_ids == 0) & (seq_index == 0), fars[head][1][:, None], 0.0)
        total = total.astype(jnp.bfloat16).reshape(2, heads, -1, HD)
        for k in range(heads):
            piece = lax.dynamic_index_in_dim(total, head_index ^ k, 1, keepdims=False)
            pair_pieces[k, head] = across(piece, k, f"out_pairs{head}_{k}")
    return (query_out, *assemble_pairs(place, heads, kv_local, pair_pieces))


def solution(mesh):
    return jax.shard_map(
        shards,
        mesh=mesh,
        in_specs=(
            P("seq", "head"),
            P("seq", "head"),
            P("seq", "head"),
            P("seq", "head"),
            P(),
            P("seq", None),
            P("seq", None),
        ),
        out_specs=(P(("seq", "head"), None), P(("seq", "head"), None), P(("seq", "head"), None)),
        check_vma=False,
    )
```
